256 devices in a mesh: slab: 8 (over z_hi, core), px: 4 (over y), py: 8 (over z_lo, x).
Axes of the slice: x: 4, y: 4, z: 8 (z_hi: 4, z_lo: 2; z = z_hi * 2 + z_lo), core: 2. Of those that a mesh axis runs over, the one named last changes fastest.
Arguments:
- feat: bfloat16 [32, 8, 64, 1024], P(None, 'px', 'py', 'slab'), may hold values from -6 to 6
- w_enc: bfloat16 [32, 32, 3, 3, 3], replicated, may hold values from -0.21875 to 0.21875
- w_down: bfloat16 [64, 32, 3, 3, 3], replicated, may hold values from -0.21875 to 0.21875
- w_dec: bfloat16 [32, 96, 3, 3, 3], replicated, may hold values from -0.125 to 0.125
- cotangent: bfloat16 [32, 8, 64, 1024], P(None, 'px', 'py', 'slab'), may hold values from -6 to 6
Outputs:
- result: bfloat16 [32, 8, 64, 1024], P(None, 'px', 'py', 'slab')
- grad_feat: bfloat16 [32, 8, 64, 1024], P(None, 'px', 'py', 'slab')
- grad_enc: float32 [32, 32, 3, 3, 3], replicated
- grad_down: float32 [64, 32, 3, 3, 3], replicated
- grad_dec: float32 [32, 96, 3, 3, 3], replicated
The draws below stay inside these ranges and needn't reach their ends.
All inputs are finite; a program needn't handle non-finite values.
Results may differ from the reference program's by a relative error of at most 0.013.
Values may be sent and summed in bfloat16 or wider, within the bound.
A program may use at most 64 MiB of HBM per device.

```python
import math
import jax
import jax.numpy as jnp
from jax import lax

C1 = 32
C2 = 64
NX = 8
NY = 64
NZ = 1024


def level_of(stream_key, extent, split, least, high):
    loudness, own = 1.0, jax.random.fold_in(stream_key, 6)
    for axis_at, blocks in split:
        draws = jnp.exp(jax.random.uniform(jax.random.fold_in(own, axis_at), (blocks,), jnp.float32, least / len(split), high / len(split)))
        loudness = loudness * jnp.repeat(draws, extent[axis_at] // blocks).reshape([-1 if axis == axis_at else 1 for axis in range(len(extent))])
    return loudness


def gaussian(own_key, shape, deviation, limit, cuts=(), kind=jnp.bfloat16):
    drawn = deviation * jax.random.normal(own_key, shape, jnp.float32)
    if cuts:
        drawn = drawn * level_of(own_key, shape, cuts, -0.22, 0.18)
    return jnp.clip(drawn, -limit, limit).astype(kind)


def setup_inputs(seed: int = 0) -> dict:
    key_list = jax.random.split(jax.random.key(seed), 6)
    return {
        "feat": gaussian(key_list[0], (C1, NX, NY, NZ), 1.0, 6.0, ((1, 4), (2, 8), (3, 8))),
        "w_enc": gaussian(key_list[1], (C1, C1, 3, 3, 3), (27 * C1) ** -0.5, 0.21875),
        "w_down": gaussian(key_list[2], (C2, C1, 3, 3, 3), (27 * C1) ** -0.5, 0.21875),
        "w_dec": gaussian(key_list[3], (C1, C1 + C2, 3, 3, 3), (27 * (C1 + C2)) ** -0.5, 0.125),
        "cotangent": gaussian(key_list[4], (C1, NX, NY, NZ), 1.0, 6.0, ((1, 4), (2, 8), (3, 8))),
    }


def conv_valid(padded, weight):
    return lax.conv_general_dilated(padded[None], weight, (1, 1, 1), 'VALID', dimension_numbers=('NCDHW', 'OIDHW', 'NCDHW'), preferred_element_type=jnp.float32)[0]

def pad_cells(field):
    return jnp.pad(field, ((0, 0), (1, 1), (1, 1), (1, 1)))

def flipped(weight):
    return jnp.flip(weight, (2, 3, 4)).swapaxes(0, 1)

def weight_grad(grad_out, padded):
    size_x, size_y, size_z = (grad_out.shape[1], grad_out.shape[2], grad_out.shape[3])
    terms = []
    for offset_x in range(3):
        for offset_y in range(3):
            for offset_z in range(3):
                piece = padded[:, offset_x:offset_x + size_x, offset_y:offset_y + size_y, offset_z:offset_z + size_z]
                terms.append(jnp.einsum('oxyz,ixyz->oi', grad_out, piece, preferred_element_type=jnp.float32))
    stacked = jnp.stack(terms)
    return stacked.reshape(3, 3, 3, stacked.shape[1], stacked.shape[2]).transpose(3, 4, 0, 1, 2)

def pool_cells(field):
    chans, size_x, size_y, size_z = field.shape
    blocks = field.astype(jnp.float32).reshape(chans, size_x // 2, 2, size_y // 2, 2, size_z // 2, 2)
    return blocks.mean(axis=(2, 4, 6)).astype(jnp.bfloat16)

def fold_cells(field):
    chans, size_x, size_y, size_z = field.shape
    return field.reshape(chans, size_x // 2, 2, size_y // 2, 2, size_z // 2, 2).sum(axis=(2, 4, 6))

def upsample(field):
    return jnp.repeat(jnp.repeat(jnp.repeat(field, 2, 1), 2, 2), 2, 3)

def silu_slope(value):
    sig = jax.nn.sigmoid(value)
    return sig * (1.0 + value * (1.0 - sig))

def reference(feat, w_enc, w_down, w_dec, cotangent):
    enc_pre = conv_valid(pad_cells(feat), w_enc)
    skip = jax.nn.silu(enc_pre).astype(jnp.bfloat16)
    pooled = pool_cells(skip)
    down_pre = conv_valid(pad_cells(pooled), w_down)
    coarse = jax.nn.silu(down_pre).astype(jnp.bfloat16)
    joined = jnp.concatenate([upsample(coarse), skip], axis=0)
    joined_pad = pad_cells(joined)
    result = conv_valid(joined_pad, w_dec).astype(jnp.bfloat16)
    grad_joined = conv_valid(pad_cells(cotangent), flipped(w_dec))
    dec_sum = weight_grad(cotangent, joined_pad)
    grad_coarse = (fold_cells(grad_joined[:C2]) * silu_slope(down_pre)).astype(jnp.bfloat16)
    grad_pooled = conv_valid(pad_cells(grad_coarse), flipped(w_down))
    down_sum = weight_grad(grad_coarse, pad_cells(pooled))
    grad_skip = ((grad_joined[C2:] + upsample(grad_pooled) * 0.125) * silu_slope(enc_pre)).astype(jnp.bfloat16)
    enc_sum = weight_grad(grad_skip, pad_cells(feat))
    grad_feat = conv_valid(pad_cells(grad_skip), flipped(w_enc)).astype(jnp.bfloat16)
    scale = 1.0 / math.sqrt(float(NX * NY * NZ))
    return (result, grad_feat, enc_sum * scale, down_sum * scale, dec_sum * scale)
```

```python
import functools
import math

import jax
import jax.numpy as jnp
from jax import lax
from jax.experimental import pallas as pl
from jax.experimental.pallas import tpu as pltpu
from jax.sharding import PartitionSpec as P

MESH = pl.DeviceIdType.MESH
BF = jnp.bfloat16
F32 = jnp.float32
L = 128
TAPS = [(kx, ky, kz) for kz in range(3) for ky in range(3) for kx in range(3)]
PLACE = [kx * 9 + ky * 3 + kz for kx, ky, kz in TAPS]
AROUND = [(dx, dy) for dx in (-1, 0, 1) for dy in (-1, 0, 1) if (dx, dy) != (0, 0)]


def dot(a, b):
    return jnp.dot(a, b, preferred_element_type=F32)


def dot_t(a, b):
    return lax.dot_general(a, b, (((1,), (1,)), ((), ())), preferred_element_type=F32)


def lanes():
    return lax.broadcasted_iota(jnp.int32, (1, L), 1)


def pair_sum(value):
    even = lax.rem(lanes(), 2) == 0
    return value + jnp.where(even, pltpu.roll(value, L - 1, 1), pltpu.roll(value, 1, 1))


def silu_slope(value):
    sig = jax.nn.sigmoid(value)
    return sig * (1.0 + value * (1.0 - sig))


class Halo:
    def __init__(self, at, sizes, field, sent, edge, sems, ny, nx, width):
        self.at, self.sizes, self.field, self.sent, self.edge = at, sizes, field, sent, edge
        self.send, self.recv = sems
        self.ny, self.nx, self.width = ny, nx, width

    def has(self, dx, dy):
        _, px, py = self.at
        _, nx, ny = self.sizes
        return (px + dx >= 0) & (px + dx < nx) & (py + dy >= 0) & (py + dy < ny)

    def plane_copy(self, index):
        dx, dy = AROUND[index]

        def spans(step, size):
            source = {-1: pl.ds(1, 1), 0: pl.ds(1, size), 1: pl.ds(size, 1)}[step]
            target = {-1: pl.ds(size + 1, 1), 0: pl.ds(1, size), 1: pl.ds(0, 1)}[step]
            return source, target

        (sx, tx), (sy, ty) = spans(dx, self.nx), spans(dy, self.ny)
        slab, px, py = self.at
        return pltpu.make_async_remote_copy(
            src_ref=self.field.at[sy, sx],
            dst_ref=self.field.at[ty, tx],
            send_sem=self.send.at[index],
            recv_sem=self.recv.at[index],
            device_id=(slab, px + dx, py + dy),
            device_id_type=MESH,
        )

    def start_plane(self):
        for index, (dx, dy) in enumerate(AROUND):
            pl.when(self.has(dx, dy))(lambda index=index: self.plane_copy(index).start())

    def wait_plane(self):
        for index, (dx, dy) in enumerate(AROUND):
            pl.when(self.has(-dx, -dy))(lambda index=index: self.plane_copy(index).wait_recv())

    def depth_copy(self, side):
        slab, px, py = self.at
        return pltpu.make_async_remote_copy(
            src_ref=self.sent.at[side],
            dst_ref=self.edge.at[side],
            send_sem=self.send.at[8 + side],
            recv_sem=self.recv.at[8 + side],
            device_id=(slab + 1 - 2 * side, px, py),
            device_id_type=MESH,
        )

    def depth_has(self, side, sending):
        up = (side == 0) == sending
        return self.at[0] < self.sizes[0] - 1 if up else self.at[0] > 0

    def start_depth(self):
        width, across = self.width, self.nx + 2
        channels = self.field.shape[2]
        place = lanes() // width

        def step(y, held):
            last, first = held
            for x in range(across):
                row = self.field[y, x].astype(F32)
                index = y * across + x
                last = jnp.where(place == index, pltpu.roll(row, lax.rem(width * index + width, L), 1), last)
                first = jnp.where(place == index, pltpu.roll(row, width * index, 1), first)
            return last, first

        zero = jnp.zeros((channels, L), F32)
        last, first = lax.fori_loop(0, self.ny + 2, step, (zero, zero))
        self.sent[0] = last.astype(BF)
        self.sent[1] = first.astype(BF)
        for side in (0, 1):
            pl.when(self.depth_has(side, True))(lambda side=side: self.depth_copy(side).start())

    def wait_depth(self):
        for side in (0, 1):
            pl.when(self.depth_has(side, False))(lambda side=side: self.depth_copy(side).wait_recv())

    def wait_sent(self):
        for index, (dx, dy) in enumerate(AROUND):
            pl.when(self.has(dx, dy))(lambda index=index: self.plane_copy(index).wait_send())
        for side in (0, 1):
            pl.when(self.depth_has(side, True))(lambda side=side: self.depth_copy(side).wait_send())

    def shift(self, span, low, high, by):
        width, across = self.width, self.nx + 2
        lane = lanes()
        left = self.edge[0, span].astype(F32)
        right = self.edge[1, span].astype(F32)

        def step(y, carry):
            for x in range(across):
                row = self.field[y, x, span].astype(F32)
                index = y * across + x
                first = pltpu.roll(left, lax.rem(L - width * index, L), 1)
                last = pltpu.roll(right, L - by - width * index, 1)
                low[y, x] = jnp.where(lane < by, first, pltpu.roll(row, by, 1)).astype(BF)
                high[y, x] = jnp.where(lane >= L - by, last, pltpu.roll(row, L - by, 1)).astype(BF)
            return carry

        lax.fori_loop(0, self.ny + 2, step, 0)


def patch(low, mid, high, y, x):
    pieces = []
    for ref in (low, mid, high):
        for ky in range(3):
            for kx in range(3):
                pieces.append(ref(y + ky, x + kx))
    return jnp.concatenate(pieces, axis=0)


def reader(ref, span=None):
    if span is None:
        return lambda y, x: ref[y, x]
    return lambda y, x: ref[y, x, span]


class Total:
    def __init__(self, at, sizes, refs, sems, owners, each):
        self.at, self.sizes, self.owners, self.each = at, sizes, owners, each
        self.terms, self.landed, self.held, self.result = refs
        self.sems = sems
        self.me = at[1] * sizes[2] + at[2]
        self.count = sizes[1] * sizes[2]

    def whole(self):
        return self.owners == self.count

    def when_owner(self, device, action):
        if self.whole():
            action()
        else:
            pl.when(device < self.owners)(action)

    def target(self, step):
        return lax.rem(self.me + step, self.count)

    def device(self, index):
        return (self.at[0], index // self.sizes[2], lax.rem(index, self.sizes[2]))

    def chunk(self, index):
        return pl.ds(index * self.each, self.each)

    def drain(self, ref, copies, sem):
        if copies:
            span = ref.at[pl.ds(0, copies)]
            pltpu.make_async_copy(span, span, self.sems.at[sem]).wait()

    def by_role(self, mine, others):
        if self.whole():
            mine()
        else:
            pl.when(self.me < self.owners)(mine)
            pl.when(self.me >= self.owners)(others)

    def start_scatter(self):
        for step in range(1, self.count):
            index = self.target(step)

            def send(step=step, index=index):
                pltpu.make_async_remote_copy(
                    src_ref=self.terms.at[self.chunk(index)],
                    dst_ref=self.landed.at[step - 1],
                    send_sem=self.sems.at[0],
                    recv_sem=self.sems.at[1],
                    device_id=self.device(index),
                    device_id_type=MESH,
                ).start()

            self.when_owner(index, send)

    def start_exchange(self):
        slab = self.at[0]

        def act():
            self.drain(self.landed, self.count - 1, 1)
            total = self.terms[self.chunk(self.me)].astype(F32)
            for step in range(self.count - 1):
                total = total + self.landed[step].astype(F32)
            self.held[slab] = total.astype(BF)
            for step in range(1, self.sizes[0]):
                pltpu.make_async_remote_copy(
                    src_ref=self.held.at[slab],
                    dst_ref=self.held.at[slab],
                    send_sem=self.sems.at[2],
                    recv_sem=self.sems.at[3],
                    device_id=(lax.rem(slab + step, self.sizes[0]), self.at[1], self.at[2]),
                    device_id_type=MESH,
                ).start()

        self.when_owner(self.me, act)

    def start_gather(self):
        def act():
            self.drain(self.held, self.sizes[0] - 1, 3)
            total = self.held[0].astype(F32)
            for step in range(1, self.sizes[0]):
                total = total + self.held[step].astype(F32)
            self.result[self.chunk(self.me)] = total.astype(BF)
            for step in range(1, self.count):
                pltpu.make_async_remote_copy(
                    src_ref=self.result.at[self.chunk(self.me)],
                    dst_ref=self.result.at[self.chunk(self.me)],
                    send_sem=self.sems.at[4],
                    recv_sem=self.sems.at[5],
                    device_id=self.device(self.target(step)),
                    device_id_type=MESH,
                ).start()

        self.when_owner(self.me, act)

    def finish(self):
        def mine():
            self.drain(self.terms, (self.owners - 1) * self.each, 0)
            self.drain(self.held, self.sizes[0] - 1, 2)
            self.drain(self.landed, self.count - 1, 4)
            self.drain(self.result, (self.owners - 1) * self.each, 5)

        def others():
            self.drain(self.terms, self.owners * self.each, 0)
            self.drain(self.result, self.owners * self.each, 5)

        self.by_role(mine, others)


def kernel(
    sizes,
    plan,
    feat_ref,
    cot_ref,
    enc_ref,
    down_ref,
    dec_ref,
    result_ref,
    grad_feat_ref,
    grad_enc_ref,
    grad_down_ref,
    grad_dec_ref,
    rows_ref,
    w_enc,
    w_enc_t,
    w_down,
    w_down_t,
    w_dec,
    w_dec_t,
    field_a,
    field_b,
    field_d,
    field_e,
    sent_a,
    sent_b,
    sent_d,
    sent_e,
    edge_a,
    edge_b,
    edge_d,
    edge_e,
    feat_low,
    feat_high,
    cot_low,
    cot_high,
    pool_low,
    pool_high,
    coarse_low,
    coarse_high,
    slope_low,
    slope_high,
    skip_low,
    skip_high,
    back_low,
    back_high,
    enc_pre,
    joined_grad,
    own_joined,
    dec_sum,
    enc_sum,
    terms_1,
    landed_1,
    held_1,
    result_1,
    terms_2,
    landed_2,
    held_2,
    result_2,
    halo_send,
    halo_recv,
    total_sems,
):
    (owners_1, each_1), (owners_2, each_2) = plan
    channels, nx, ny, _ = feat_ref.shape
    ncy = ny // 2
    coarse_channels = down_ref.shape[2]
    joined_channels = channels + coarse_channels
    at = (lax.axis_index("slab"), lax.axis_index("px"), lax.axis_index("py"))
    count = sizes[1] * sizes[2]
    sum_1 = Total(at, sizes, (terms_1, landed_1, held_1, result_1), total_sems.at[0], owners_1, each_1)
    sum_2 = Total(at, sizes, (terms_2, landed_2, held_2, result_2), total_sems.at[1], owners_2, each_2)

    for ref in (field_a, field_b, field_d, field_e, edge_a, edge_b, edge_d, edge_e):
        ref[...] = jnp.zeros_like(ref)

    barrier = pltpu.get_barrier_semaphore()
    for step in range(1, count):
        pl.semaphore_signal(barrier, inc=1, device_id=sum_1.device(sum_1.target(step)), device_id_type=MESH)
    for step in range(1, sizes[0]):
        other = lax.rem(at[0] + step, sizes[0])
        pl.semaphore_signal(barrier, inc=1, device_id=(other, at[1], at[2]), device_id_type=MESH)

    terms_1[...] = jnp.zeros_like(terms_1)
    terms_2[...] = jnp.zeros_like(terms_2)

    across = nx * ny
    for at_channel, ref in ((0, feat_ref), (channels, cot_ref)):
        rows_ref[...] = ref[...].astype(F32).reshape(channels * across, L)
        for x in range(nx):
            for y in range(ny):
                row = rows_ref[pl.ds(x * ny + y, channels, stride=across), :]
                field_a[y + 1, x + 1, at_channel : at_channel + channels] = row.astype(BF)

    pl.semaphore_wait(barrier, count - 1 + sizes[0] - 1)

    def halo(index, field, sent, edge, rows, columns, width):
        sems = (halo_send.at[index], halo_recv.at[index])
        return Halo(at, sizes, field, sent, edge, sems, rows, columns, width)

    halo_a = halo(0, field_a, sent_a, edge_a, ny, nx, 1)
    halo_b = halo(1, field_b, sent_b, edge_b, ncy, 1, 2)
    halo_d = halo(2, field_d, sent_d, edge_d, ncy, 1, 2)
    halo_e = halo(3, field_e, sent_e, edge_e, ny, nx, 1)

    halo_a.start_plane()
    w_enc[...] = jnp.concatenate([enc_ref[p] for p in PLACE], axis=1)
    w_enc_t[...] = jnp.concatenate([enc_ref[26 - p] for p in PLACE], axis=0).T
    w_down[...] = jnp.concatenate([down_ref[p] for p in PLACE], axis=0).T
    w_down_t[...] = jnp.concatenate([down_ref[26 - p] for p in PLACE], axis=1)
    w_dec[...] = jnp.concatenate([dec_ref[p] for p in PLACE], axis=1)
    w_dec_t[...] = jnp.concatenate([dec_ref[26 - p] for p in PLACE], axis=0).T
    halo_a.wait_plane()
    halo_a.start_depth()
    halo_a.wait_depth()
    head, tail = slice(0, channels), slice(channels, 2 * channels)
    halo_a.shift(head, feat_low, feat_high, 1)
    halo_a.shift(tail, cot_low, cot_high, 1)
    feat_of = (reader(feat_low), reader(field_a, head), reader(feat_high))
    cot_of = (reader(cot_low), reader(field_a, tail), reader(cot_high))

    def fine(of, y):
        return jnp.concatenate([patch(*of, y, x) for x in range(nx)], axis=1)

    def span_of(y):
        return pl.ds(pl.multiple_of(y * (nx * L), nx * L), nx * L)

    def encode(yc, carry):
        pooled = jnp.zeros((channels, L), F32)
        for sub in range(2):
            y = 2 * yc + sub
            pre = dot(w_enc[...], fine(feat_of, y))
            enc_pre[:, span_of(y)] = pre
            skip = (pre * jax.nn.sigmoid(pre)).astype(BF)
            own_joined[coarse_channels:, span_of(y)] = skip
            for x in range(nx):
                row = skip[:, x * L : (x + 1) * L]
                field_e[y + 1, x + 1, head] = row
                pooled = pooled + row.astype(F32)
        field_b[yc + 1, 1] = (pair_sum(pooled) * 0.125).astype(BF)
        return carry

    lax.fori_loop(0, ncy, encode, 0)

    halo_b.start_plane()

    def back(y, carry):
        joined_grad[:, span_of(y)] = dot(w_dec_t[...], fine(cot_of, y))
        return carry

    lax.fori_loop(0, ny, back, 0)
    halo_b.wait_plane()
    halo_b.start_depth()
    halo_b.wait_depth()
    halo_b.shift(slice(0, channels), pool_low, pool_high, 2)
    pool_of = (reader(pool_low), reader(field_b), reader(pool_high))
    pooled_patch = jnp.concatenate([patch(*pool_of, yc, 0) for yc in range(ncy)], axis=1)
    down_pre = dot(w_down[...], pooled_patch)
    coarse = (down_pre * jax.nn.sigmoid(down_pre)).astype(BF)
    slope = silu_slope(down_pre)
    low_half, high_half = slice(0, coarse_channels), slice(coarse_channels, 2 * coarse_channels)
    grads = []
    for yc in range(ncy):
        field_d[yc + 1, 1, low_half] = coarse[:, yc * L : (yc + 1) * L]
        folded = jnp.zeros((coarse_channels, L), F32)
        for sub in range(2):
            for x in range(nx):
                cell = ((2 * yc + sub) * nx + x) * L
                folded = folded + joined_grad[:coarse_channels, cell : cell + L]
                own_joined[:coarse_channels, cell : cell + L] = coarse[:, yc * L : (yc + 1) * L]
        grad = (pair_sum(folded) * slope[:, yc * L : (yc + 1) * L]).astype(BF)
        field_d[yc + 1, 1, high_half] = grad
        grads.append(grad)

    halo_d.start_plane()
    down_sum = dot_t(pooled_patch, jnp.concatenate(grads, axis=1)) * 0.5
    half = down_sum.shape[0] // 2
    dec_sum[...] = jnp.zeros_like(dec_sum)

    def dec_step(y, carry):
        dec_sum[...] += dot_t(fine(cot_of, y), own_joined[:, span_of(y)])
        return carry

    lax.fori_loop(0, ny, dec_step, 0)
    dec_tiles = dec_sum.shape[0] // 16
    down_tiles = half // 16
    terms_1[0:dec_tiles, :, 0:joined_channels] = dec_sum[...].astype(BF).reshape(dec_tiles, 16, joined_channels)
    paired = jnp.concatenate([down_sum[:half], down_sum[half:]], axis=1)
    terms_1[dec_tiles : dec_tiles + down_tiles] = paired.astype(BF).reshape(down_tiles, 16, L)
    halo_d.wait_plane()
    halo_d.start_depth()
    sum_1.start_scatter()
    halo_d.wait_depth()
    halo_d.shift(high_half, slope_low, slope_high, 2)
    slope_of = (reader(slope_low), reader(field_d, high_half), reader(slope_high))
    slope_patch = jnp.concatenate([patch(*slope_of, yc, 0) for yc in range(ncy)], axis=1)
    grad_pooled = dot(w_down_t[...], slope_patch) * 0.125
    for yc in range(ncy):
        for sub in range(2):
            for x in range(nx):
                cell = ((2 * yc + sub) * nx + x) * L
                total = joined_grad[coarse_channels:, cell : cell + L] + grad_pooled[:, yc * L : (yc + 1) * L]
                grad = (total * silu_slope(enc_pre[:, cell : cell + L])).astype(BF)
                field_e[2 * yc + sub + 1, x + 1, tail] = grad

    halo_e.start_plane()
    enc_sum[...] = jnp.zeros_like(enc_sum)

    def enc_step(y, carry):
        own = jnp.concatenate([field_e[y + 1, x + 1, tail] for x in range(nx)], axis=1)
        enc_sum[...] += dot_t(own, fine(feat_of, y))
        return carry

    lax.fori_loop(0, ny, enc_step, 0)
    wide = enc_sum.shape[1]
    for h in range(channels // 16):
        for at_lane in range(0, wide, L):
            size = min(L, wide - at_lane)
            piece = enc_sum[16 * h : 16 * h + 16, at_lane : at_lane + size]
            terms_2[h * pl.cdiv(wide, L) + at_lane // L, :, 0:size] = piece.astype(BF)
    sum_2.start_scatter()
    halo_d.shift(low_half, coarse_low, coarse_high, 1)
    halo_e.wait_plane()
    halo_e.start_depth()
    sum_1.start_exchange()
    sum_2.start_exchange()
    halo_e.wait_depth()
    halo_e.shift(tail, back_low, back_high, 1)
    halo_e.shift(head, skip_low, skip_high, 1)
    sum_1.start_gather()
    sum_2.start_gather()

    back_of = (reader(back_low), reader(field_e, tail), reader(back_high))

    def put(y, value):
        for x in range(nx):
            rows_ref[pl.ds(x * ny + y, channels, stride=across), :] = value[:, x * L : (x + 1) * L]

    def flush(ref):
        ref[...] = rows_ref[...].reshape(channels, nx, ny, L).astype(BF)

    def feat_step(y, carry):
        put(y, dot(w_enc_t[...], fine(back_of, y)))
        return carry

    lax.fori_loop(0, ny, feat_step, 0)
    flush(grad_feat_ref)

    coarse_of = (reader(coarse_low), reader(field_d, low_half), reader(coarse_high))
    skip_of = (reader(skip_low), reader(field_e, head), reader(skip_high))

    def result_step(yc, carry):
        for sub in range(2):
            columns = []
            for x in range(nx):
                pieces = []
                for kz in range(3):
                    for ky in range(3):
                        for kx in range(3):
                            pieces.append(coarse_of[kz](yc + (sub + ky + 1) // 2, (x + kx + 1) // 2))
                            pieces.append(skip_of[kz](2 * yc + sub + ky, x + kx))
                columns.append(jnp.concatenate(pieces, axis=0))
            put(2 * yc + sub, dot(w_dec[...], jnp.concatenate(columns, axis=1)))
        return carry

    lax.fori_loop(0, ncy, result_step, 0)
    flush(result_ref)

    scale = 1.0 / math.sqrt(float(nx * ny * L * sizes[0] * sizes[1] * sizes[2]))
    sum_1.finish()
    tiles = channels // 16
    for index, (place) in enumerate(PLACE):
        held = result_1[index * tiles : (index + 1) * tiles].astype(F32).reshape(channels, L)
        grad_dec_ref[26 - place] = held[:, :joined_channels] * scale
    both = result_1[dec_tiles : dec_tiles + down_tiles].astype(F32).reshape(half, L) * scale
    whole = jnp.concatenate([both[:, :coarse_channels], both[:, coarse_channels:]], axis=0)
    for index, place in enumerate(PLACE):
        grad_down_ref[place] = whole[index * channels : (index + 1) * channels]
    sum_2.finish()
    across_tiles = pl.cdiv(wide, L)
    for index, place in enumerate(PLACE):
        lane = index * channels
        for h in range(channels // 16):
            tile = result_2[h * across_tiles + lane // L].astype(F32)
            grad_enc_ref[place, 16 * h : 16 * h + 16] = tile[:, lane % L : lane % L + channels] * scale
    for each in (halo_a, halo_b, halo_d, halo_e):
        each.wait_sent()


def shards(sizes, feat, w_enc, w_down, w_dec, cotangent):
    channels, nx, ny, nz = feat.shape
    coarse_channels = w_down.shape[0]
    joined_channels = channels + coarse_channels
    ncy = ny // 2
    count = sizes[1] * sizes[2]
    tiles_1 = 27 * channels // 16 + 27 * channels // 32
    tiles_2 = channels // 16 * pl.cdiv(27 * channels, L)
    owners_1, owners_2 = count, min(count, tiles_2)
    each_1, each_2 = pl.cdiv(tiles_1, owners_1), pl.cdiv(tiles_2, owners_2)

    def taps(weight, order):
        return weight.transpose(2, 3, 4, *order).reshape(27, weight.shape[order[0]], weight.shape[order[1]])

    def vmem(*shape, dtype=BF):
        return pltpu.VMEM(shape, dtype)

    def fine(c):
        return vmem(ny + 2, nx + 2, c, L)

    def small(c):
        return vmem(ncy + 2, 3, c, L)

    c1, c2, cj = channels, coarse_channels, joined_channels
    scratch = [
        vmem(c1 * nx * ny, L, dtype=F32),
        vmem(c1, 27 * c1),
        vmem(c1, 27 * c1),
        vmem(c2, 27 * c1),
        vmem(c1, 27 * c2),
        vmem(c1, 27 * cj),
        vmem(cj, 27 * c1),
        fine(2 * c1),
        small(c1),
        small(2 * c2),
        fine(2 * c1),
    ]
    scratch += [vmem(2, c, L) for c in (2 * c1, c1, 2 * c2, 2 * c1)] * 2
    scratch += [fine(c1)] * 4 + [small(c1)] * 2 + [small(c2)] * 4 + [fine(c1)] * 4
    scratch += [
        vmem(c1, nx * ny * L, dtype=F32),
        vmem(cj, nx * ny * L, dtype=F32),
        vmem(cj, nx * ny * L),
        vmem(27 * c1, cj, dtype=F32),
        vmem(c1, 27 * c1, dtype=F32),
    ]
    for owners, each in ((owners_1, each_1), (owners_2, each_2)):
        scratch += [
            vmem(owners * each, 16, L),
            vmem(count - 1, each, 16, L),
            vmem(sizes[0], each, 16, L),
            vmem(owners * each, 16, L),
        ]
    scratch += [
        pltpu.SemaphoreType.DMA((4, 10)),
        pltpu.SemaphoreType.DMA((4, 10)),
        pltpu.SemaphoreType.DMA((2, 6)),
    ]
    whole = pl.BlockSpec(memory_space=pltpu.VMEM)
    shapes = [
        jax.ShapeDtypeStruct(feat.shape, BF),
        jax.ShapeDtypeStruct(feat.shape, BF),
        jax.ShapeDtypeStruct((27, c1, c1), F32),
        jax.ShapeDtypeStruct((27, c1, c2), F32),
        jax.ShapeDtypeStruct((27, c1, cj), F32),
    ]
    result, grad_feat, grad_enc, grad_down, grad_dec = pl.pallas_call(
        functools.partial(kernel, sizes, ((owners_1, each_1), (owners_2, each_2))),
        out_shape=shapes,
        in_specs=[whole] * 5,
        out_specs=[whole] * 5,
        scratch_shapes=scratch,
        compiler_params=pltpu.CompilerParams(
            collective_id=0, has_side_effects=True, vmem_limit_bytes=56 << 20
        ),
    )(feat, cotangent, taps(w_enc, (0, 1)), taps(w_down, (1, 0)), taps(w_dec, (0, 1)))

    def untaps(value, order):
        return value.reshape(3, 3, 3, *value.shape[1:]).transpose(*order, 0, 1, 2)

    return (
        result,
        grad_feat,
        untaps(grad_enc, (3, 4)),
        untaps(grad_down, (4, 3)),
        untaps(grad_dec, (3, 4)),
    )


def solution(mesh):
    sizes = tuple(mesh.shape[axis] for axis in ("slab", "px", "py"))
    placed = P(None, "px", "py", "slab")
    return jax.shard_map(
        functools.partial(shards, sizes),
        mesh=mesh,
        in_specs=(placed, P(), P(), P(), placed),
        out_specs=(placed, placed, P(), P(), P()),
        check_vma=False,
    )
```

```python
import functools
import itertools
import math

import jax
import jax.numpy as jnp
from jax import lax
from jax.experimental import pallas as pl
from jax.experimental.pallas import tpu as pltpu
from jax.sharding import PartitionSpec as P

EXCHANGES = ("feat", "cot", "pool", "skip", "slope", "coarse", "back")
FINE = (0, 1, 3, 6)
MESH = pl.DeviceIdType.MESH
BF = jnp.bfloat16
F32 = jnp.float32
L = 128
TAPS = [(kx, ky, kz) for kz in range(3) for ky in range(3) for kx in range(3)]
PLACE = [kx * 9 + ky * 3 + kz for kx, ky, kz in TAPS]
AROUND = sorted(
    (step for step in itertools.product((-1, 0, 1), repeat=3) if any(step)),
    key=lambda step: -sum(map(abs, step)),
)


def dot(a, b):
    return jnp.dot(a, b, preferred_element_type=F32)


def dot_t(a, b):
    return lax.dot_general(a, b, (((1,), (1,)), ((), ())), preferred_element_type=F32)


def lanes():
    return lax.broadcasted_iota(jnp.int32, (1, L), 1)


def pair_sum(value):
    even = lax.rem(lanes(), 2) == 0
    return value + jnp.where(even, pltpu.roll(value, L - 1, 1), pltpu.roll(value, 1, 1))


def silu_slope(value):
    sig = jax.nn.sigmoid(value)
    return sig * (1.0 + value * (1.0 - sig))


def near(at, sizes, step, sign=1):
    inside = True
    for place, size, move in zip(at, sizes, step):
        if move:
            inside = inside & (place + sign * move >= 0) & (place + sign * move < size)
    return inside


class Halo:
    def __init__(self, at, sizes, field, sent, edge, sems, ny, nx, width):
        self.at, self.sizes, self.field, self.sent, self.edge = at, sizes, field, sent, edge
        self.send, self.recv = sems
        self.ny, self.nx, self.width = ny, nx, width

    def has(self, step, sign=1):
        return near(self.at, self.sizes, step, sign)

    def copy(self, index):
        ds, dx, dy = AROUND[index]

        def spans(step, size):
            source = {-1: pl.ds(1, 1), 0: pl.ds(1, size), 1: pl.ds(size, 1)}[step]
            target = {-1: pl.ds(size + 1, 1), 0: pl.ds(1, size), 1: pl.ds(0, 1)}[step]
            return source, target

        if ds == 0:
            (sx, tx), (sy, ty) = spans(dx, self.nx), spans(dy, self.ny)
            source, target = self.field.at[sy, sx], self.field.at[ty, tx]
        else:
            side = (1 - ds) // 2
            source, target = self.sent.at[side], self.edge.at[side, (1 - dy) * 3 + 1 - dx]
        return pltpu.make_async_remote_copy(
            src_ref=source,
            dst_ref=target,
            send_sem=self.send.at[index],
            recv_sem=self.recv.at[index],
            device_id=tuple(a + d for a, d in zip(self.at, AROUND[index])),
            device_id_type=MESH,
        )

    def start_where(self, plane):
        for index, step in enumerate(AROUND):
            if (step[0] == 0) == plane:
                pl.when(self.has(step))(lambda index=index: self.copy(index).start())

    def place(self, group, cell):
        return self.width * ((group * self.ny + cell[0]) * self.nx + cell[1])

    def start(self):
        self.start_where(True)
        width = self.width
        lane = lanes() // width
        last = first = jnp.zeros((16, L), F32)
        for cell in itertools.product(range(self.ny), range(self.nx)):
            row = self.field[cell[0] + 1, cell[1] + 1].astype(F32)
            for group in range(row.shape[0] // 16):
                piece = row[16 * group : 16 * group + 16]
                place = self.place(group, cell)
                here = lane == place // width
                last = jnp.where(here, pltpu.roll(piece, (place + width) % L, 1), last)
                first = jnp.where(here, pltpu.roll(piece, place, 1), first)
        self.sent[0] = last.astype(BF)
        self.sent[1] = first.astype(BF)
        self.start_where(False)

    def clear(self):
        zero = jnp.zeros(self.field.shape[2:], BF)
        for y in range(self.ny + 2):
            for x in range(self.nx + 2):
                if y in (0, self.ny + 1) or x in (0, self.nx + 1):
                    self.field[y, x] = zero
        self.edge[...] = jnp.zeros_like(self.edge)

    def wait(self):
        for index, step in enumerate(AROUND):
            pl.when(self.has(step, -1))(lambda index=index: self.copy(index).wait_recv())

    def wait_sent(self):
        for index, step in enumerate(AROUND):
            pl.when(self.has(step))(lambda index=index: self.copy(index).wait_send())

    def shift(self, low, high, by):
        ny, nx = self.ny, self.nx
        lane = lanes()
        for y in range(ny + 2):
            for x in range(nx + 2):
                row = self.field[y, x].astype(F32)
                (dy, oy), (dx, ox) = divmod(y + ny - 1, ny), divmod(x + nx - 1, nx)
                left = self.edge[0, dy * 3 + dx].astype(F32)
                right = self.edge[1, dy * 3 + dx].astype(F32)
                places = [self.place(group, (oy, ox)) for group in range(row.shape[0] // 16)]
                first = jnp.concatenate([pltpu.roll(left, (L - at) % L, 1) for at in places])
                last = jnp.concatenate([pltpu.roll(right, (2 * L - by - at) % L, 1) for at in places])
                low[y, x] = jnp.where(lane < by, first, pltpu.roll(row, by, 1)).astype(BF)
                high[y, x] = jnp.where(lane >= L - by, last, pltpu.roll(row, L - by, 1)).astype(BF)


def patch(low, mid, high, y, x):
    pieces = []
    for ref in (low, mid, high):
        for ky in range(3):
            for kx in range(3):
                pieces.append(ref(y + ky, x + kx))
    return jnp.concatenate(pieces, axis=0)


def reader(ref):
    return lambda y, x: ref[y, x]


class Total:
    def __init__(self, at, sizes, refs, sems, owners, each):
        self.at, self.sizes, self.owners, self.each = at, sizes, owners, each
        self.terms, self.landed, self.held, self.result = refs
        self.sems = sems
        self.me = at[1] * sizes[2] + at[2]
        self.count = sizes[1] * sizes[2]

    def whole(self):
        return self.owners == self.count

    def when_owner(self, device, action):
        if self.whole():
            action()
        else:
            pl.when(device < self.owners)(action)

    def target(self, step):
        return lax.rem(self.me + step, self.count)

    def device(self, index):
        return (self.at[0], index // self.sizes[2], lax.rem(index, self.sizes[2]))

    def chunk(self, index):
        return pl.ds(index * self.each, self.each)

    def drain(self, ref, copies, sem):
        if copies:
            span = ref.at[pl.ds(0, copies)]
            pltpu.make_async_copy(span, span, self.sems.at[sem]).wait()

    def by_role(self, mine, others):
        if self.whole():
            mine()
        else:
            pl.when(self.me < self.owners)(mine)
            pl.when(self.me >= self.owners)(others)

    def start_scatter(self):
        for step in range(1, self.count):
            index = self.target(step)

            def send(step=step, index=index):
                pltpu.make_async_remote_copy(
                    src_ref=self.terms.at[self.chunk(index)],
                    dst_ref=self.landed.at[step - 1],
                    send_sem=self.sems.at[0],
                    recv_sem=self.sems.at[1],
                    device_id=self.device(index),
                    device_id_type=MESH,
                ).start()

            self.when_owner(index, send)

    def start_exchange(self):
        slab = self.at[0]

        def act():
            self.drain(self.landed, self.count - 1, 1)
            total = self.terms[self.chunk(self.me)].astype(F32)
            for step in range(self.count - 1):
                total = total + self.landed[step].astype(F32)
            self.held[slab] = total.astype(BF)
            for step in range(1, self.sizes[0]):
                pltpu.make_async_remote_copy(
                    src_ref=self.held.at[slab],
                    dst_ref=self.held.at[slab],
                    send_sem=self.sems.at[2],
                    recv_sem=self.sems.at[3],
                    device_id=(lax.rem(slab + step, self.sizes[0]), self.at[1], self.at[2]),
                    device_id_type=MESH,
                ).start()

        self.when_owner(self.me, act)

    def start_gather(self):
        def act():
            self.drain(self.held, self.sizes[0] - 1, 3)
            total = self.held[0].astype(F32)
            for step in range(1, self.sizes[0]):
                total = total + self.held[step].astype(F32)
            self.result[self.chunk(self.me)] = total.astype(BF)
            for step in range(1, self.count):
                pltpu.make_async_remote_copy(
                    src_ref=self.result.at[self.chunk(self.me)],
                    dst_ref=self.result.at[self.chunk(self.me)],
                    send_sem=self.sems.at[4],
                    recv_sem=self.sems.at[5],
                    device_id=self.device(self.target(step)),
                    device_id_type=MESH,
                ).start()

        self.when_owner(self.me, act)

    def finish(self):
        def mine():
            self.drain(self.terms, (self.owners - 1) * self.each, 0)
            self.drain(self.held, self.sizes[0] - 1, 2)
            self.drain(self.landed, self.count - 1, 4)
            self.drain(self.result, (self.owners - 1) * self.each, 5)

        def others():
            self.drain(self.terms, self.owners * self.each, 0)
            self.drain(self.result, self.owners * self.each, 5)

        self.by_role(mine, others)


def kernel(
    sizes,
    plan,
    feat_in,
    cot_in,
    enc_in,
    down_in,
    dec_in,
    result_out,
    grad_feat_out,
    tiles_1_out,
    tiles_2_out,
    feat_ref,
    cot_ref,
    enc_ref,
    down_ref,
    dec_ref,
    result_ref,
    grad_feat_ref,
    rows_ref,
    w_enc,
    w_enc_t,
    w_down,
    w_down_t,
    w_dec,
    w_dec_t,
    fields,
    lows,
    highs,
    sents,
    edges,
    enc_pre,
    joined_grad,
    own_joined,
    dec_sum,
    enc_sum,
    total_refs_1,
    total_refs_2,
    halo_send,
    halo_recv,
    total_sems,
    sems,
):
    (owners_1, each_1), (owners_2, each_2) = plan
    channels, nx, ny, _ = feat_ref.shape
    ncy = ny // 2
    coarse_channels = down_ref.shape[2]
    joined_channels = channels + coarse_channels
    at = (lax.axis_index("slab"), lax.axis_index("px"), lax.axis_index("py"))
    count = sizes[1] * sizes[2]
    sum_1 = Total(at, sizes, total_refs_1, total_sems.at[0], owners_1, each_1)
    sum_2 = Total(at, sizes, total_refs_2, total_sems.at[1], owners_2, each_2)

    arrive = [
        pltpu.make_async_copy(source, target, sems.at[index])
        for index, (source, target) in enumerate(
            zip((feat_in, cot_in, enc_in, down_in, dec_in), (feat_ref, cot_ref, enc_ref, down_ref, dec_ref))
        )
    ]
    for copy in arrive:
        copy.start()

    def halo(index, rows, columns, width):
        refs = (fields[index], sents[index], edges[index])
        return Halo(at, sizes, *refs, (halo_send.at[index], halo_recv.at[index]), rows, columns, width)

    halos = [halo(index, *((ny, nx, 1) if index in FINE else (ncy, 1, 2))) for index in range(7)]
    of_feat, of_cot, of_pool, of_skip, of_slope, of_coarse, of_back = halos
    for each in halos:
        each.clear()

    barrier = pltpu.get_barrier_semaphore()
    for step in range(1, count):
        pl.semaphore_signal(barrier, inc=1, device_id=sum_1.device(sum_1.target(step)), device_id_type=MESH)
    for step in range(1, sizes[0]):
        other = lax.rem(at[0] + step, sizes[0])
        pl.semaphore_signal(barrier, inc=1, device_id=(other, at[1], at[2]), device_id_type=MESH)
    greeted = count - 1 + sizes[0] - 1
    for step in AROUND:
        if step[0] and (step[1] or step[2]):
            there = near(at, sizes, step)
            greeted = greeted + there.astype(jnp.int32)
            target = tuple(a + d for a, d in zip(at, step))

            @pl.when(there)
            def _(target=target):
                pl.semaphore_signal(barrier, inc=1, device_id=target, device_id_type=MESH)

    across = nx * ny
    for index, ref in ((0, feat_ref), (1, cot_ref)):
        arrive[index].wait()
        rows_ref[...] = ref[...].astype(F32).reshape(channels * across, L)
        for x in range(nx):
            for y in range(ny):
                row = rows_ref[pl.ds(x * ny + y, channels, stride=across), :]
                fields[index][y + 1, x + 1] = row.astype(BF)
    terms_1, terms_2 = total_refs_1[0], total_refs_2[0]
    terms_1[...] = jnp.zeros_like(terms_1)
    terms_2[...] = jnp.zeros_like(terms_2)
    pl.semaphore_wait(barrier, greeted)

    of_feat.start()
    of_cot.start()
    for copy in arrive[2:]:
        copy.wait()
    w_enc[...] = jnp.concatenate([enc_ref[p] for p in PLACE], axis=1)
    w_enc_t[...] = jnp.concatenate([enc_ref[26 - p] for p in PLACE], axis=0).T
    w_down[...] = jnp.concatenate([down_ref[p] for p in PLACE], axis=0).T
    w_down_t[...] = jnp.concatenate([down_ref[26 - p] for p in PLACE], axis=1)
    w_dec[...] = jnp.concatenate([dec_ref[p] for p in PLACE], axis=1)
    w_dec_t[...] = jnp.concatenate([dec_ref[26 - p] for p in PLACE], axis=0).T

    def moved(index, by):
        halos[index].shift(lows[index], highs[index], by)
        return reader(lows[index]), reader(fields[index]), reader(highs[index])

    def fine(of, y):
        return jnp.concatenate([patch(*of, y, x) for x in range(nx)], axis=1)

    def span_of(y):
        return pl.ds(pl.multiple_of(y * (nx * L), nx * L), nx * L)

    of_feat.wait()
    feat_of = moved(0, 1)

    def encode(yc, carry):
        pooled = jnp.zeros((channels, L), F32)
        for sub in range(2):
            y = 2 * yc + sub
            pre = dot(w_enc[...], fine(feat_of, y))
            enc_pre[:, span_of(y)] = pre
            skip = (pre * jax.nn.sigmoid(pre)).astype(BF)
            own_joined[coarse_channels:, span_of(y)] = skip
            for x in range(nx):
                row = skip[:, x * L : (x + 1) * L]
                fields[3][y + 1, x + 1] = row
                pooled = pooled + row.astype(F32)
        fields[2][yc + 1, 1] = (pair_sum(pooled) * 0.125).astype(BF)
        return carry

    lax.fori_loop(0, ncy, encode, 0)

    of_pool.start()
    of_skip.start()
    of_cot.wait()
    cot_of = moved(1, 1)

    def back(y, carry):
        joined_grad[:, span_of(y)] = dot(w_dec_t[...], fine(cot_of, y))
        return carry

    lax.fori_loop(0, ny, back, 0)
    of_pool.wait()
    pool_of = moved(2, 2)
    pooled_patch = jnp.concatenate([patch(*pool_of, yc, 0) for yc in range(ncy)], axis=1)
    down_pre = dot(w_down[...], pooled_patch)
    slope = silu_slope(down_pre)
    grads = []
    for yc in range(ncy):
        folded = jnp.zeros((coarse_channels, L), F32)
        for sub in range(2):
            for x in range(nx):
                cell = ((2 * yc + sub) * nx + x) * L
                folded = folded + joined_grad[:coarse_channels, cell : cell + L]
        grad = (pair_sum(folded) * slope[:, yc * L : (yc + 1) * L]).astype(BF)
        fields[4][yc + 1, 1] = grad
        grads.append(grad)

    of_slope.start()
    coarse = (down_pre * jax.nn.sigmoid(down_pre)).astype(BF)
    for yc in range(ncy):
        own = coarse[:, yc * L : (yc + 1) * L]
        fields[5][yc + 1, 1] = own
        for sub in range(2):
            for x in range(nx):
                cell = ((2 * yc + sub) * nx + x) * L
                own_joined[:coarse_channels, cell : cell + L] = own
    of_coarse.start()
    down_sum = dot_t(pooled_patch, jnp.concatenate(grads, axis=1)) * 0.5
    half = down_sum.shape[0] // 2
    dec_sum[...] = jnp.zeros_like(dec_sum)

    def dec_step(y, carry):
        dec_sum[...] += dot_t(fine(cot_of, y), own_joined[:, span_of(y)])
        return carry

    lax.fori_loop(0, ny, dec_step, 0)
    dec_tiles = dec_sum.shape[0] // 16
    down_tiles = half // 16
    terms_1[0:dec_tiles, :, 0:joined_channels] = dec_sum[...].astype(BF).reshape(dec_tiles, 16, joined_channels)
    paired = jnp.concatenate([down_sum[:half], down_sum[half:]], axis=1)
    terms_1[dec_tiles : dec_tiles + down_tiles] = paired.astype(BF).reshape(down_tiles, 16, L)
    sum_1.start_scatter()
    of_slope.wait()
    slope_of = moved(4, 2)
    slope_patch = jnp.concatenate([patch(*slope_of, yc, 0) for yc in range(ncy)], axis=1)
    grad_pooled = dot(w_down_t[...], slope_patch) * 0.125
    for yc in range(ncy):
        for sub in range(2):
            for x in range(nx):
                cell = ((2 * yc + sub) * nx + x) * L
                total = joined_grad[coarse_channels:, cell : cell + L] + grad_pooled[:, yc * L : (yc + 1) * L]
                grad = (total * silu_slope(enc_pre[:, cell : cell + L])).astype(BF)
                fields[6][2 * yc + sub + 1, x + 1] = grad

    enc_sum[...] = jnp.zeros_like(enc_sum)

    def enc_step(y, carry):
        own = jnp.concatenate([fields[6][y + 1, x + 1] for x in range(nx)], axis=1)
        enc_sum[...] += dot_t(own, fine(feat_of, y))
        return carry

    lax.fori_loop(0, ny, enc_step, 0)
    wide = enc_sum.shape[1]
    for h in range(channels // 16):
        for at_lane in range(0, wide, L):
            size = min(L, wide - at_lane)
            piece = enc_sum[16 * h : 16 * h + 16, at_lane : at_lane + size]
            terms_2[h * pl.cdiv(wide, L) + at_lane // L, :, 0:size] = piece.astype(BF)
    sum_2.start_scatter()
    of_back.start()
    sum_1.start_exchange()

    def put(y, value):
        for x in range(nx):
            rows_ref[pl.ds(x * ny + y, channels, stride=across), :] = value[:, x * L : (x + 1) * L]

    leave = [
        pltpu.make_async_copy(source, target, sems.at[index])
        for index, (source, target) in enumerate(
            zip(
                (result_ref, grad_feat_ref, total_refs_1[3], total_refs_2[3]),
                (result_out, grad_feat_out, tiles_1_out, tiles_2_out),
            )
        )
    ]

    def flush(ref, copy):
        ref[...] = rows_ref[...].reshape(channels, nx, ny, L).astype(BF)
        copy.start()

    of_coarse.wait()
    coarse_of = moved(5, 1)
    of_skip.wait()
    skip_of = moved(3, 1)

    def result_step(yc, carry):
        for sub in range(2):
            columns = []
            for x in range(nx):
                pieces = []
                for kz in range(3):
                    for ky in range(3):
                        for kx in range(3):
                            pieces.append(coarse_of[kz](yc + (sub + ky + 1) // 2, (x + kx + 1) // 2))
                            pieces.append(skip_of[kz](2 * yc + sub + ky, x + kx))
                columns.append(jnp.concatenate(pieces, axis=0))
            put(2 * yc + sub, dot(w_dec[...], jnp.concatenate(columns, axis=1)))
        return carry

    lax.fori_loop(0, ncy, result_step, 0)
    flush(result_ref, leave[0])
    sum_2.start_exchange()
    of_back.wait()
    back_of = moved(6, 1)
    sum_1.start_gather()

    def feat_step(y, carry):
        put(y, dot(w_enc_t[...], fine(back_of, y)))
        return carry

    lax.fori_loop(0, ny, feat_step, 0)
    sum_2.start_gather()
    flush(grad_feat_ref, leave[1])
    for each in halos:
        each.wait_sent()
    sum_1.finish()
    leave[2].start()
    sum_2.finish()
    leave[3].start()
    for copy in leave:
        copy.wait()


def unpack(
    scale,
    result_in,
    grad_feat_in,
    tiles_1_in,
    tiles_2_in,
    result_out,
    grad_feat_out,
    grad_enc_out,
    grad_down_out,
    grad_dec_out,
    result,
    grad_feat,
    tiles_1,
    tiles_2,
    grad_enc,
    grad_down,
    grad_dec,
    sems,
):
    arrived = [
        pltpu.make_async_copy(source, target, sems.at[index])
        for index, (source, target) in enumerate(zip((tiles_1_in, tiles_2_in, result_in, grad_feat_in), (tiles_1, tiles_2, result, grad_feat)))
    ]
    for copy in arrived:
        copy.start()
    ends = (result_out, grad_feat_out, grad_enc_out, grad_down_out, grad_dec_out)
    leaving = [
        pltpu.make_async_copy(source, target, sems.at[4 + index])
        for index, (source, target) in enumerate(zip((result, grad_feat, grad_enc, grad_down, grad_dec), ends))
    ]
    channels, coarse_channels = grad_down.shape[1:]
    joined_channels = grad_dec.shape[2]
    tiles = channels // 16
    dec_tiles = 27 * tiles
    arrived[0].wait()
    for index, place in enumerate(PLACE):
        held = tiles_1[index * tiles : (index + 1) * tiles].astype(F32).reshape(channels, L)
        grad_dec[26 - place] = held[:, :joined_channels] * scale
    leaving[4].start()
    half = 27 * channels // 2
    both = tiles_1[dec_tiles : dec_tiles + half // 16].astype(F32).reshape(half, L) * scale
    whole = jnp.concatenate([both[:, :coarse_channels], both[:, coarse_channels:]], axis=0)
    for index, place in enumerate(PLACE):
        grad_down[place] = whole[index * channels : (index + 1) * channels]
    leaving[3].start()
    arrived[1].wait()
    across_tiles = pl.cdiv(27 * channels, L)
    for index, place in enumerate(PLACE):
        lane = index * channels
        for h in range(tiles):
            tile = tiles_2[h * across_tiles + lane // L].astype(F32)
            grad_enc[place, 16 * h : 16 * h + 16] = tile[:, lane % L : lane % L + channels] * scale
    leaving[2].start()
    for index in (0, 1):
        arrived[2 + index].wait()
        leaving[index].start()
    for copy in leaving:
        copy.wait()


def shards(sizes, feat, w_enc, w_down, w_dec, cotangent):
    channels, nx, ny, nz = feat.shape
    coarse_channels = w_down.shape[0]
    joined_channels = channels + coarse_channels
    ncy = ny // 2
    count = sizes[1] * sizes[2]
    tiles_1 = 27 * channels // 16 + 27 * channels // 32
    tiles_2 = channels // 16 * pl.cdiv(27 * channels, L)
    owners_1, owners_2 = count, min(count, tiles_2)
    each_1, each_2 = pl.cdiv(tiles_1, owners_1), pl.cdiv(tiles_2, owners_2)

    def taps(weight, order):
        return weight.transpose(2, 3, 4, *order).reshape(27, weight.shape[order[0]], weight.shape[order[1]])

    def vmem(*shape, dtype=BF):
        return pltpu.VMEM(shape, dtype)

    def fine(c):
        return vmem(ny + 2, nx + 2, c, L)

    def small(c):
        return vmem(ncy + 2, 3, c, L)

    c1, c2, cj = channels, coarse_channels, joined_channels
    shaped = [fine(c1), fine(c1), small(c1), fine(c1), small(c2), small(c2), fine(c1)]
    scratch = [vmem(*feat.shape)] * 2
    scratch += [vmem(27, c1, c) for c in (c1, c2, cj)]
    scratch += [vmem(*feat.shape)] * 2
    scratch += [
        vmem(c1 * nx * ny, L, dtype=F32),
        vmem(c1, 27 * c1),
        vmem(c1, 27 * c1),
        vmem(c2, 27 * c1),
        vmem(c1, 27 * c2),
        vmem(c1, 27 * cj),
        vmem(cj, 27 * c1),
    ]
    scratch += [shaped] * 3
    scratch += [[vmem(2, 16, L)] * 7, [vmem(2, 9, 16, L)] * 7]
    scratch += [
        vmem(c1, nx * ny * L, dtype=F32),
        vmem(cj, nx * ny * L, dtype=F32),
        vmem(cj, nx * ny * L),
        vmem(27 * c1, cj, dtype=F32),
        vmem(c1, 27 * c1, dtype=F32),
    ]
    for owners, each in ((owners_1, each_1), (owners_2, each_2)):
        scratch.append(
            [
                vmem(owners * each, 16, L),
                vmem(count - 1, each, 16, L),
                vmem(sizes[0], each, 16, L),
                vmem(owners * each, 16, L),
            ]
        )
    scratch += [
        pltpu.SemaphoreType.DMA((7, len(AROUND))),
        pltpu.SemaphoreType.DMA((7, len(AROUND))),
        pltpu.SemaphoreType.DMA((2, 6)),
        pltpu.SemaphoreType.DMA((5,)),
    ]
    apart = pl.BlockSpec(memory_space=pl.ANY)
    fields = [jax.ShapeDtypeStruct(feat.shape, BF)] * 2
    grads = [jax.ShapeDtypeStruct((27, c1, c), F32) for c in (c1, c2, cj)]
    held_tiles = (owners_1 * each_1, owners_2 * each_2)
    tiles = [jax.ShapeDtypeStruct((size, 16, L), BF) for size in held_tiles]
    held = pl.pallas_call(
        functools.partial(kernel, sizes, ((owners_1, each_1), (owners_2, each_2))),
        out_shape=fields + tiles,
        in_specs=[apart] * 5,
        out_specs=[apart] * 4,
        scratch_shapes=scratch,
        compiler_params=pltpu.CompilerParams(
            collective_id=0, has_side_effects=True, vmem_limit_bytes=56 << 20
        ),
    )(feat, cotangent, taps(w_enc, (0, 1)), taps(w_down, (1, 0)), taps(w_dec, (0, 1)))
    scale = 1.0 / math.sqrt(float(nx * ny * nz * sizes[0] * sizes[1] * sizes[2]))
    result, grad_feat, grad_enc, grad_down, grad_dec = pl.pallas_call(
        functools.partial(unpack, scale),
        out_shape=fields + grads,
        in_specs=[apart] * 4,
        out_specs=[apart] * 5,
        scratch_shapes=[pltpu.VMEM(each.shape, each.dtype) for each in fields + tiles + grads]
        + [pltpu.SemaphoreType.DMA((9,))],
        compiler_params=pltpu.CompilerParams(vmem_limit_bytes=60 << 20),
    )(*held)

    def untaps(value, order):
        return value.reshape(3, 3, 3, *value.shape[1:]).transpose(*order, 0, 1, 2)

    return (
        result,
        grad_feat,
        untaps(grad_enc, (3, 4)),
        untaps(grad_down, (4, 3)),
        untaps(grad_dec, (3, 4)),
    )


def solution(mesh):
    sizes = tuple(mesh.shape[axis] for axis in ("slab", "px", "py"))
    placed = P(None, "px", "py", "slab")
    return jax.shard_map(
        functools.partial(shards, sizes),
        mesh=mesh,
        in_specs=(placed, P(), P(), P(), placed),
        out_specs=(placed, placed, P(), P(), P()),
        check_vma=False,
    )
```

```python
import functools
import itertools
import math

import jax
import jax.numpy as jnp
from jax import lax
from jax.experimental import pallas as pl
from jax.experimental.pallas import tpu as pltpu
from jax.sharding import PartitionSpec as P

EXCHANGES = ("feat", "cot", "pool", "skip", "slope", "coarse", "back")
FINE = (0, 1, 3, 6)
MESH = pl.DeviceIdType.MESH
BF = jnp.bfloat16
F32 = jnp.float32
L = 128
TAPS = [(kx, ky, kz) for kz in range(3) for ky in range(3) for kx in range(3)]
PLACE = [kx * 9 + ky * 3 + kz for kx, ky, kz in TAPS]
AROUND = sorted(
    (step for step in itertools.product((-1, 0, 1), repeat=3) if any(step)),
    key=lambda step: -sum(map(abs, step)),
)


def dot(a, b):
    return jnp.dot(a, b, preferred_element_type=F32)


def dot_t(a, b):
    return lax.dot_general(a, b, (((1,), (1,)), ((), ())), preferred_element_type=F32)


def lanes():
    return lax.broadcasted_iota(jnp.int32, (1, L), 1)


def pair_sum(value):
    even = lax.rem(lanes(), 2) == 0
    return value + jnp.where(even, pltpu.roll(value, L - 1, 1), pltpu.roll(value, 1, 1))


def silu_slope(value):
    sig = jax.nn.sigmoid(value)
    return sig * (1.0 + value * (1.0 - sig))


def near(at, sizes, step, sign=1):
    inside = True
    for place, size, move in zip(at, sizes, step):
        if move:
            inside = inside & (place + sign * move >= 0) & (place + sign * move < size)
    return inside


class Halo:
    def __init__(self, at, sizes, field, sent, edge, sems, ny, nx, width):
        self.at, self.sizes, self.field, self.sent, self.edge = at, sizes, field, sent, edge
        self.send, self.recv = sems
        self.ny, self.nx, self.width = ny, nx, width

    def has(self, step, sign=1):
        return near(self.at, self.sizes, step, sign)

    def copy(self, index):
        ds, dx, dy = AROUND[index]

        def spans(step, size):
            source = {-1: pl.ds(1, 1), 0: pl.ds(1, size), 1: pl.ds(size, 1)}[step]
            target = {-1: pl.ds(size + 1, 1), 0: pl.ds(1, size), 1: pl.ds(0, 1)}[step]
            return source, target

        if ds == 0:
            (sx, tx), (sy, ty) = spans(dx, self.nx), spans(dy, self.ny)
            source, target = self.field.at[sy, sx], self.field.at[ty, tx]
        else:
            side = (1 - ds) // 2
            source, target = self.sent.at[side], self.edge.at[side, (1 - dy) * 3 + 1 - dx]
        return pltpu.make_async_remote_copy(
            src_ref=source,
            dst_ref=target,
            send_sem=self.send.at[index],
            recv_sem=self.recv.at[index],
            device_id=tuple(a + d for a, d in zip(self.at, AROUND[index])),
            device_id_type=MESH,
        )

    def start_where(self, plane):
        for index, step in enumerate(AROUND):
            if (step[0] == 0) == plane:
                pl.when(self.has(step))(lambda index=index: self.copy(index).start())

    def place(self, group, cell):
        return self.width * ((group * self.ny + cell[0]) * self.nx + cell[1])

    def start(self):
        self.start_where(True)
        width = self.width
        lane = lanes() // width
        last = first = jnp.zeros((16, L), F32)
        for cell in itertools.product(range(self.ny), range(self.nx)):
            row = self.field[cell[0] + 1, cell[1] + 1].astype(F32)
            for group in range(row.shape[0] // 16):
                piece = row[16 * group : 16 * group + 16]
                place = self.place(group, cell)
                here = lane == place // width
                last = jnp.where(here, pltpu.roll(piece, (place + width) % L, 1), last)
                first = jnp.where(here, pltpu.roll(piece, place, 1), first)
        self.sent[0] = last.astype(BF)
        self.sent[1] = first.astype(BF)
        self.start_where(False)

    def clear(self):
        zero = jnp.zeros(self.field.shape[2:], BF)
        for y in range(self.ny + 2):
            for x in range(self.nx + 2):
                if y in (0, self.ny + 1) or x in (0, self.nx + 1):
                    self.field[y, x] = zero
        self.edge[...] = jnp.zeros_like(self.edge)

    def wait(self):
        for index, step in enumerate(AROUND):
            pl.when(self.has(step, -1))(lambda index=index: self.copy(index).wait_recv())

    def wait_sent(self):
        for index, step in enumerate(AROUND):
            pl.when(self.has(step))(lambda index=index: self.copy(index).wait_send())

    def shift(self, low, high, by):
        ny, nx = self.ny, self.nx
        lane = lanes()
        for y in range(ny + 2):
            for x in range(nx + 2):
                row = self.field[y, x].astype(F32)
                (dy, oy), (dx, ox) = divmod(y + ny - 1, ny), divmod(x + nx - 1, nx)
                left = self.edge[0, dy * 3 + dx].astype(F32)
                right = self.edge[1, dy * 3 + dx].astype(F32)
                places = [self.place(group, (oy, ox)) for group in range(row.shape[0] // 16)]
                first = jnp.concatenate([pltpu.roll(left, (L - at) % L, 1) for at in places])
                last = jnp.concatenate([pltpu.roll(right, (2 * L - by - at) % L, 1) for at in places])
                low[y, x] = jnp.where(lane < by, first, pltpu.roll(row, by, 1)).astype(BF)
                high[y, x] = jnp.where(lane >= L - by, last, pltpu.roll(row, L - by, 1)).astype(BF)


def patch(low, mid, high, y, x):
    pieces = []
    for ref in (low, mid, high):
        for ky in range(3):
            for kx in range(3):
                pieces.append(ref(y + ky, x + kx))
    return jnp.concatenate(pieces, axis=0)


def reader(ref):
    return lambda y, x: ref[y, x]


class Total:
    def __init__(self, at, sizes, refs, sems, owners, each):
        self.at, self.sizes, self.owners, self.each = at, sizes, owners, each
        self.terms, self.landed, self.held, self.result = refs
        self.sems = sems
        self.me = at[1] * sizes[2] + at[2]
        self.count = sizes[1] * sizes[2]

    def whole(self):
        return self.owners == self.count

    def when_owner(self, device, action):
        if self.whole():
            action()
        else:
            pl.when(device < self.owners)(action)

    def target(self, step):
        return lax.rem(self.me + step, self.count)

    def device(self, index):
        return (self.at[0], index // self.sizes[2], lax.rem(index, self.sizes[2]))

    def chunk(self, index):
        return pl.ds(index * self.each, self.each)

    def drain(self, ref, copies, sem):
        if copies:
            span = ref.at[pl.ds(0, copies)]
            pltpu.make_async_copy(span, span, self.sems.at[sem]).wait()

    def by_role(self, mine, others):
        if self.whole():
            mine()
        else:
            pl.when(self.me < self.owners)(mine)
            pl.when(self.me >= self.owners)(others)

    def start_scatter(self):
        for step in range(1, self.count):
            index = self.target(step)

            def send(step=step, index=index):
                pltpu.make_async_remote_copy(
                    src_ref=self.terms.at[self.chunk(index)],
                    dst_ref=self.landed.at[step - 1],
                    send_sem=self.sems.at[0],
                    recv_sem=self.sems.at[1],
                    device_id=self.device(index),
                    device_id_type=MESH,
                ).start()

            self.when_owner(index, send)

    def start_exchange(self):
        slab = self.at[0]

        def act():
            self.drain(self.landed, self.count - 1, 1)
            total = self.terms[self.chunk(self.me)].astype(F32)
            for step in range(self.count - 1):
                total = total + self.landed[step].astype(F32)
            self.held[slab] = total.astype(BF)
            for step in range(1, self.sizes[0]):
                pltpu.make_async_remote_copy(
                    src_ref=self.held.at[slab],
                    dst_ref=self.held.at[slab],
                    send_sem=self.sems.at[2],
                    recv_sem=self.sems.at[3],
                    device_id=(lax.rem(slab + step, self.sizes[0]), self.at[1], self.at[2]),
                    device_id_type=MESH,
                ).start()

        self.when_owner(self.me, act)

    def start_gather(self):
        def act():
            self.drain(self.held, self.sizes[0] - 1, 3)
            total = self.held[0].astype(F32)
            for step in range(1, self.sizes[0]):
                total = total + self.held[step].astype(F32)
            self.result[self.chunk(self.me)] = total.astype(BF)
            for step in range(1, self.count):
                pltpu.make_async_remote_copy(
                    src_ref=self.result.at[self.chunk(self.me)],
                    dst_ref=self.result.at[self.chunk(self.me)],
                    send_sem=self.sems.at[4],
                    recv_sem=self.sems.at[5],
                    device_id=self.device(self.target(step)),
                    device_id_type=MESH,
                ).start()

        self.when_owner(self.me, act)

    def finish(self):
        def mine():
            self.drain(self.terms, (self.owners - 1) * self.each, 0)
            self.drain(self.held, self.sizes[0] - 1, 2)
            self.drain(self.landed, self.count - 1, 4)
            self.drain(self.result, (self.owners - 1) * self.each, 5)

        def others():
            self.drain(self.terms, self.owners * self.each, 0)
            self.drain(self.result, self.owners * self.each, 5)

        self.by_role(mine, others)


def kernel(
    sizes,
    plan,
    feat_in,
    cot_in,
    enc_in,
    down_in,
    dec_in,
    result_out,
    grad_feat_out,
    tiles_1_out,
    tiles_2_out,
    feat_ref,
    cot_ref,
    enc_ref,
    down_ref,
    dec_ref,
    result_ref,
    grad_feat_ref,
    rows_ref,
    w_enc,
    w_enc_t,
    w_down,
    w_down_t,
    w_dec,
    w_dec_t,
    fields,
    lows,
    highs,
    sents,
    edges,
    enc_pre,
    joined_grad,
    own_joined,
    dec_sum,
    dec_skip_sum,
    enc_sum,
    total_refs_1,
    total_refs_2,
    halo_send,
    halo_recv,
    total_sems,
    sems,
):
    (owners_1, each_1), (owners_2, each_2) = plan
    channels, nx, ny, _ = feat_ref.shape
    ncy = ny // 2
    coarse_channels = down_ref.shape[2]
    joined_channels = channels + coarse_channels
    at = (lax.axis_index("slab"), lax.axis_index("px"), lax.axis_index("py"))
    count = sizes[1] * sizes[2]
    sum_1 = Total(at, sizes, total_refs_1, total_sems.at[0], owners_1, each_1)
    sum_2 = Total(at, sizes, total_refs_2, total_sems.at[1], owners_2, each_2)

    arrive = [
        pltpu.make_async_copy(source, target, sems.at[index])
        for index, (source, target) in enumerate(
            zip((feat_in, cot_in, enc_in, down_in, dec_in), (feat_ref, cot_ref, enc_ref, down_ref, dec_ref))
        )
    ]
    for copy in arrive:
        copy.start()

    def halo(index, rows, columns, width):
        refs = (fields[index], sents[index], edges[index])
        return Halo(at, sizes, *refs, (halo_send.at[index], halo_recv.at[index]), rows, columns, width)

    halos = [halo(index, *((ny, nx, 1) if index in FINE else (ncy, 1, 2))) for index in range(7)]
    of_feat, of_cot, of_pool, of_skip, of_slope, of_coarse, of_back = halos
    for each in halos:
        each.clear()

    barrier = pltpu.get_barrier_semaphore()
    for step in range(1, count):
        pl.semaphore_signal(barrier, inc=1, device_id=sum_1.device(sum_1.target(step)), device_id_type=MESH)
    for step in range(1, sizes[0]):
        other = lax.rem(at[0] + step, sizes[0])
        pl.semaphore_signal(barrier, inc=1, device_id=(other, at[1], at[2]), device_id_type=MESH)
    greeted = count - 1 + sizes[0] - 1
    for step in AROUND:
        if step[0] and (step[1] or step[2]):
            there = near(at, sizes, step)
            greeted = greeted + there.astype(jnp.int32)
            target = tuple(a + d for a, d in zip(at, step))

            @pl.when(there)
            def _(target=target):
                pl.semaphore_signal(barrier, inc=1, device_id=target, device_id_type=MESH)

    across = nx * ny
    for index, ref in ((0, feat_ref), (1, cot_ref)):
        arrive[index].wait()
        rows_ref[...] = ref[...].astype(F32).reshape(channels * across, L)
        for x in range(nx):
            for y in range(ny):
                row = rows_ref[pl.ds(x * ny + y, channels, stride=across), :]
                fields[index][y + 1, x + 1] = row.astype(BF)
    terms_1, terms_2 = total_refs_1[0], total_refs_2[0]
    terms_1[...] = jnp.zeros_like(terms_1)
    terms_2[...] = jnp.zeros_like(terms_2)
    pl.semaphore_wait(barrier, greeted)

    of_feat.start()
    of_cot.start()
    for copy in arrive[2:]:
        copy.wait()
    w_enc[...] = jnp.concatenate([enc_ref[p] for p in PLACE], axis=1)
    w_enc_t[...] = jnp.concatenate([enc_ref[26 - p] for p in PLACE], axis=0).T
    w_down[...] = jnp.concatenate([down_ref[p] for p in PLACE], axis=0).T
    w_down_t[...] = jnp.concatenate([down_ref[26 - p] for p in PLACE], axis=1)
    w_dec[...] = jnp.concatenate([dec_ref[p] for p in PLACE], axis=1)
    w_dec_t[...] = jnp.concatenate([dec_ref[26 - p] for p in PLACE], axis=0).T

    def moved(index, by):
        halos[index].shift(lows[index], highs[index], by)
        return reader(lows[index]), reader(fields[index]), reader(highs[index])

    def fine(of, y):
        return jnp.concatenate([patch(*of, y, x) for x in range(nx)], axis=1)

    def span_of(y):
        return pl.ds(pl.multiple_of(y * (nx * L), nx * L), nx * L)

    of_feat.wait()
    feat_of = moved(0, 1)

    def encode(yc, carry):
        pooled = jnp.zeros((channels, L), F32)
        for sub in range(2):
            y = 2 * yc + sub
            pre = dot(w_enc[...], fine(feat_of, y))
            enc_pre[:, span_of(y)] = pre
            skip = (pre * jax.nn.sigmoid(pre)).astype(BF)
            own_joined[coarse_channels:, span_of(y)] = skip
            for x in range(nx):
                row = skip[:, x * L : (x + 1) * L]
                fields[3][y + 1, x + 1] = row
                pooled = pooled + row.astype(F32)
        fields[2][yc + 1, 1] = (pair_sum(pooled) * 0.125).astype(BF)
        return carry

    lax.fori_loop(0, ncy, encode, 0)

    of_pool.start()
    of_skip.start()
    of_cot.wait()
    cot_of = moved(1, 1)

    def back(y, carry):
        joined_grad[:, span_of(y)] = dot(w_dec_t[...], fine(cot_of, y))
        return carry

    lax.fori_loop(0, ny, back, 0)
    dec_skip_sum[...] = jnp.zeros_like(dec_skip_sum)

    def dec_skip_step(y, carry):
        dec_skip_sum[...] += dot_t(fine(cot_of, y), own_joined[coarse_channels:, span_of(y)])
        return carry

    lax.fori_loop(0, ny, dec_skip_step, 0)
    held_rows = 7 * channels
    quarters = [dec_skip_sum[q * held_rows : (q + 1) * held_rows] for q in range(3)]
    quarters.append(jnp.concatenate([dec_skip_sum[3 * held_rows :], jnp.zeros((channels, channels), F32)], axis=0))
    skip_tiles = jnp.concatenate(quarters, axis=1).astype(BF).reshape(held_rows // 16, 16, L)
    terms_2[terms_2.shape[0] - held_rows // 16 :] = skip_tiles
    of_pool.wait()
    pool_of = moved(2, 2)
    pooled_patch = jnp.concatenate([patch(*pool_of, yc, 0) for yc in range(ncy)], axis=1)
    down_pre = dot(w_down[...], pooled_patch)
    slope = silu_slope(down_pre)
    grads = []
    for yc in range(ncy):
        folded = jnp.zeros((coarse_channels, L), F32)
        for sub in range(2):
            for x in range(nx):
                cell = ((2 * yc + sub) * nx + x) * L
                folded = folded + joined_grad[:coarse_channels, cell : cell + L]
        grad = (pair_sum(folded) * slope[:, yc * L : (yc + 1) * L]).astype(BF)
        fields[4][yc + 1, 1] = grad
        grads.append(grad)

    of_slope.start()
    coarse = (down_pre * jax.nn.sigmoid(down_pre)).astype(BF)
    for yc in range(ncy):
        own = coarse[:, yc * L : (yc + 1) * L]
        fields[5][yc + 1, 1] = own
        for sub in range(2):
            for x in range(nx):
                cell = ((2 * yc + sub) * nx + x) * L
                own_joined[:coarse_channels, cell : cell + L] = own
    of_coarse.start()
    down_sum = dot_t(pooled_patch, jnp.concatenate(grads, axis=1)) * 0.5
    half = down_sum.shape[0] // 2
    dec_sum[...] = jnp.zeros_like(dec_sum)

    def dec_step(y, carry):
        dec_sum[...] += dot_t(fine(cot_of, y), own_joined[:coarse_channels, span_of(y)])
        return carry

    lax.fori_loop(0, ny, dec_step, 0)
    tiles = half // 16
    for index, value in enumerate((dec_sum[...], down_sum)):
        paired = jnp.concatenate([value[:half], value[half:]], axis=1)
        terms_1[index * tiles : (index + 1) * tiles] = paired.astype(BF).reshape(tiles, 16, L)
    sum_1.start_scatter()
    of_slope.wait()
    slope_of = moved(4, 2)
    slope_patch = jnp.concatenate([patch(*slope_of, yc, 0) for yc in range(ncy)], axis=1)
    grad_pooled = dot(w_down_t[...], slope_patch) * 0.125
    for yc in range(ncy):
        for sub in range(2):
            for x in range(nx):
                cell = ((2 * yc + sub) * nx + x) * L
                total = joined_grad[coarse_channels:, cell : cell + L] + grad_pooled[:, yc * L : (yc + 1) * L]
                grad = (total * silu_slope(enc_pre[:, cell : cell + L])).astype(BF)
                fields[6][2 * yc + sub + 1, x + 1] = grad

    enc_sum[...] = jnp.zeros_like(enc_sum)

    def enc_step(y, carry):
        own = jnp.concatenate([fields[6][y + 1, x + 1] for x in range(nx)], axis=1)
        enc_sum[...] += dot_t(own, fine(feat_of, y))
        return carry

    lax.fori_loop(0, ny, enc_step, 0)
    wide = enc_sum.shape[1]
    for h in range(channels // 16):
        for at_lane in range(0, wide, L):
            size = min(L, wide - at_lane)
            piece = enc_sum[16 * h : 16 * h + 16, at_lane : at_lane + size]
            terms_2[h * pl.cdiv(wide, L) + at_lane // L, :, 0:size] = piece.astype(BF)
    sum_2.start_scatter()
    of_back.start()
    def put(y, value):
        for x in range(nx):
            rows_ref[pl.ds(x * ny + y, channels, stride=across), :] = value[:, x * L : (x + 1) * L]

    leave = [
        pltpu.make_async_copy(source, target, sems.at[index])
        for index, (source, target) in enumerate(
            zip(
                (result_ref, grad_feat_ref, total_refs_1[3], total_refs_2[3]),
                (result_out, grad_feat_out, tiles_1_out, tiles_2_out),
            )
        )
    ]

    def flush(ref, copy):
        ref[...] = rows_ref[...].reshape(channels, nx, ny, L).astype(BF)
        copy.start()

    of_coarse.wait()
    coarse_of = moved(5, 1)
    of_skip.wait()
    skip_of = moved(3, 1)

    sum_1.start_exchange()
    def result_step(yc, carry):
        for sub in range(2):
            columns = []
            for x in range(nx):
                pieces = []
                for kz in range(3):
                    for ky in range(3):
                        for kx in range(3):
                            pieces.append(coarse_of[kz](yc + (sub + ky + 1) // 2, (x + kx + 1) // 2))
                            pieces.append(skip_of[kz](2 * yc + sub + ky, x + kx))
                columns.append(jnp.concatenate(pieces, axis=0))
            put(2 * yc + sub, dot(w_dec[...], jnp.concatenate(columns, axis=1)))
        return carry

    lax.fori_loop(0, ncy, result_step, 0)
    sum_2.start_exchange()
    flush(result_ref, leave[0])
    sum_1.start_gather()
    of_back.wait()
    back_of = moved(6, 1)
    def feat_step(y, carry):
        put(y, dot(w_enc_t[...], fine(back_of, y)))
        return carry

    lax.fori_loop(0, ny, feat_step, 0)
    sum_2.start_gather()
    flush(grad_feat_ref, leave[1])

    for each in halos:
        each.wait_sent()
    sum_1.finish()
    leave[2].start()
    sum_2.finish()
    leave[3].start()
    for copy in leave:
        copy.wait()


def unpack(
    scale,
    result_in,
    grad_feat_in,
    tiles_1_in,
    tiles_2_in,
    result_out,
    grad_feat_out,
    grad_enc_out,
    grad_down_out,
    grad_dec_out,
    result,
    grad_feat,
    tiles_1,
    tiles_2,
    grad_enc,
    grad_down,
    grad_dec,
    sems,
):
    arrived = [
        pltpu.make_async_copy(source, target, sems.at[index])
        for index, (source, target) in enumerate(zip((tiles_1_in, tiles_2_in, result_in, grad_feat_in), (tiles_1, tiles_2, result, grad_feat)))
    ]
    for copy in arrived:
        copy.start()
    ends = (result_out, grad_feat_out, grad_enc_out, grad_down_out, grad_dec_out)
    leaving = [
        pltpu.make_async_copy(source, target, sems.at[4 + index])
        for index, (source, target) in enumerate(zip((result, grad_feat, grad_enc, grad_down, grad_dec), ends))
    ]
    channels, coarse_channels = grad_down.shape[1:]
    tiles = channels // 16
    half = 27 * channels // 2

    def unpaired(index):
        span = tiles_1[index * (half // 16) : (index + 1) * (half // 16)]
        both = span.astype(F32).reshape(half, L) * scale
        return jnp.concatenate([both[:, :coarse_channels], both[:, coarse_channels:]], axis=0)

    arrived[0].wait()
    whole = unpaired(1)
    for index, place in enumerate(PLACE):
        grad_down[place] = whole[index * channels : (index + 1) * channels]
    leaving[3].start()
    whole = unpaired(0)
    arrived[1].wait()
    first = tiles_2.shape[0] - 7 * tiles
    for index, place in enumerate(PLACE):
        quarter, row = divmod(index, 7)
        span = tiles_2[first + row * tiles : first + (row + 1) * tiles]
        skip = span.astype(F32).reshape(channels, L)[:, quarter * channels : (quarter + 1) * channels]
        rows = whole[index * channels : (index + 1) * channels]
        grad_dec[26 - place] = jnp.concatenate([rows, skip * scale], axis=1)
    leaving[4].start()
    across_tiles = pl.cdiv(27 * channels, L)
    for index, place in enumerate(PLACE):
        lane = index * channels
        for h in range(tiles):
            tile = tiles_2[h * across_tiles + lane // L].astype(F32)
            grad_enc[place, 16 * h : 16 * h + 16] = tile[:, lane % L : lane % L + channels] * scale
    leaving[2].start()
    for index in (0, 1):
        arrived[2 + index].wait()
        leaving[index].start()
    for copy in leaving:
        copy.wait()


def shards(sizes, feat, w_enc, w_down, w_dec, cotangent):
    channels, nx, ny, nz = feat.shape
    coarse_channels = w_down.shape[0]
    joined_channels = channels + coarse_channels
    ncy = ny // 2
    count = sizes[1] * sizes[2]
    tiles_1 = 2 * (27 * channels // 32)
    tiles_2 = channels // 16 * pl.cdiv(27 * channels, L) + 7 * channels // 16
    each_1, each_2 = pl.cdiv(tiles_1, count), pl.cdiv(tiles_2, count)
    owners_1, owners_2 = pl.cdiv(tiles_1, each_1), pl.cdiv(tiles_2, each_2)

    def taps(weight, order):
        return weight.transpose(2, 3, 4, *order).reshape(27, weight.shape[order[0]], weight.shape[order[1]])

    def vmem(*shape, dtype=BF):
        return pltpu.VMEM(shape, dtype)

    def fine(c):
        return vmem(ny + 2, nx + 2, c, L)

    def small(c):
        return vmem(ncy + 2, 3, c, L)

    c1, c2, cj = channels, coarse_channels, joined_channels
    shaped = [fine(c1), fine(c1), small(c1), fine(c1), small(c2), small(c2), fine(c1)]
    scratch = [vmem(*feat.shape)] * 2
    scratch += [vmem(27, c1, c) for c in (c1, c2, cj)]
    scratch += [vmem(*feat.shape)] * 2
    scratch += [
        vmem(c1 * nx * ny, L, dtype=F32),
        vmem(c1, 27 * c1),
        vmem(c1, 27 * c1),
        vmem(c2, 27 * c1),
        vmem(c1, 27 * c2),
        vmem(c1, 27 * cj),
        vmem(cj, 27 * c1),
    ]
    scratch += [shaped] * 3
    scratch += [[vmem(2, 16, L)] * 7, [vmem(2, 9, 16, L)] * 7]
    scratch += [
        vmem(c1, nx * ny * L, dtype=F32),
        vmem(cj, nx * ny * L, dtype=F32),
        vmem(cj, nx * ny * L),
        vmem(27 * c1, c2, dtype=F32),
        vmem(27 * c1, c1, dtype=F32),
        vmem(c1, 27 * c1, dtype=F32),
    ]
    for owners, each in ((owners_1, each_1), (owners_2, each_2)):
        scratch.append(
            [
                vmem(owners * each, 16, L),
                vmem(count - 1, each, 16, L),
                vmem(sizes[0], each, 16, L),
                vmem(owners * each, 16, L),
            ]
        )
    scratch += [
        pltpu.SemaphoreType.DMA((7, len(AROUND))),
        pltpu.SemaphoreType.DMA((7, len(AROUND))),
        pltpu.SemaphoreType.DMA((2, 6)),
        pltpu.SemaphoreType.DMA((5,)),
    ]
    apart = pl.BlockSpec(memory_space=pl.ANY)
    fields = [jax.ShapeDtypeStruct(feat.shape, BF)] * 2
    grads = [jax.ShapeDtypeStruct((27, c1, c), F32) for c in (c1, c2, cj)]
    held_tiles = (owners_1 * each_1, owners_2 * each_2)
    tiles = [jax.ShapeDtypeStruct((size, 16, L), BF) for size in held_tiles]
    held = pl.pallas_call(
        functools.partial(kernel, sizes, ((owners_1, each_1), (owners_2, each_2))),
        out_shape=fields + tiles,
        in_specs=[apart] * 5,
        out_specs=[apart] * 4,
        scratch_shapes=scratch,
        compiler_params=pltpu.CompilerParams(
            collective_id=0, has_side_effects=True, vmem_limit_bytes=56 << 20
        ),
    )(feat, cotangent, taps(w_enc, (0, 1)), taps(w_down, (1, 0)), taps(w_dec, (0, 1)))
    scale = 1.0 / math.sqrt(float(nx * ny * nz * sizes[0] * sizes[1] * sizes[2]))
    result, grad_feat, grad_enc, grad_down, grad_dec = pl.pallas_call(
        functools.partial(unpack, scale),
        out_shape=fields + grads,
        in_specs=[apart] * 4,
        out_specs=[apart] * 5,
        scratch_shapes=[pltpu.VMEM(each.shape, each.dtype) for each in fields + tiles + grads]
        + [pltpu.SemaphoreType.DMA((9,))],
        compiler_params=pltpu.CompilerParams(vmem_limit_bytes=60 << 20),
    )(*held)

    def untaps(value, order):
        return value.reshape(3, 3, 3, *value.shape[1:]).transpose(*order, 0, 1, 2)

    return (
        result,
        grad_feat,
        untaps(grad_enc, (3, 4)),
        untaps(grad_down, (4, 3)),
        untaps(grad_dec, (3, 4)),
    )


def solution(mesh):
    sizes = tuple(mesh.shape[axis] for axis in ("slab", "px", "py"))
    placed = P(None, "px", "py", "slab")
    return jax.shard_map(
        functools.partial(shards, sizes),
        mesh=mesh,
        in_specs=(placed, P(), P(), P(), placed),
        out_specs=(placed, placed, P(), P(), P()),
        check_vma=False,
    )
```

```python
import functools
import itertools
import math

import jax
import jax.numpy as jnp
from jax import lax
from jax.experimental import pallas as pl
from jax.experimental.pallas import tpu as pltpu
from jax.sharding import PartitionSpec as P

EXCHANGES = ("feat", "cot", "pool", "skip", "slope", "coarse", "back")
FINE = (0, 1, 3, 6)
MESH = pl.DeviceIdType.MESH
BF = jnp.bfloat16
F32 = jnp.float32
L = 128
TAPS = [(kx, ky, kz) for kz in range(3) for ky in range(3) for kx in range(3)]
PLACE = [kx * 9 + ky * 3 + kz for kx, ky, kz in TAPS]
AROUND = sorted(
    (step for step in itertools.product((-1, 0, 1), repeat=3) if any(step)),
    key=lambda step: -sum(map(abs, step)),
)


def dot(a, b):
    return jnp.dot(a, b, preferred_element_type=F32)


def dot_t(a, b):
    return lax.dot_general(a, b, (((1,), (1,)), ((), ())), preferred_element_type=F32)


def lanes():
    return lax.broadcasted_iota(jnp.int32, (1, L), 1)


def pair_sum(value):
    even = lax.rem(lanes(), 2) == 0
    return value + jnp.where(even, pltpu.roll(value, L - 1, 1), pltpu.roll(value, 1, 1))


def silu_slope(value):
    sig = jax.nn.sigmoid(value)
    return sig * (1.0 + value * (1.0 - sig))


def near(at, sizes, step, sign=1):
    inside = True
    for place, size, move in zip(at, sizes, step):
        if move:
            inside = inside & (place + sign * move >= 0) & (place + sign * move < size)
    return inside


class Halo:
    def __init__(self, at, sizes, field, sent, edge, sems, ny, nx, width):
        self.at, self.sizes, self.field, self.sent, self.edge = at, sizes, field, sent, edge
        self.send, self.recv = sems
        self.ny, self.nx, self.width = ny, nx, width

    def has(self, step, sign=1):
        return near(self.at, self.sizes, step, sign)

    def copy(self, index):
        ds, dx, dy = AROUND[index]

        def spans(step, size):
            source = {-1: pl.ds(1, 1), 0: pl.ds(1, size), 1: pl.ds(size, 1)}[step]
            target = {-1: pl.ds(size + 1, 1), 0: pl.ds(1, size), 1: pl.ds(0, 1)}[step]
            return source, target

        if ds == 0:
            (sx, tx), (sy, ty) = spans(dx, self.nx), spans(dy, self.ny)
            source, target = self.field.at[sy, sx], self.field.at[ty, tx]
        else:
            side = (1 - ds) // 2
            source, target = self.sent.at[side], self.edge.at[side, (1 - dy) * 3 + 1 - dx]
        return pltpu.make_async_remote_copy(
            src_ref=source,
            dst_ref=target,
            send_sem=self.send.at[index],
            recv_sem=self.recv.at[index],
            device_id=tuple(a + d for a, d in zip(self.at, AROUND[index])),
            device_id_type=MESH,
        )

    def start_where(self, plane):
        for index, step in enumerate(AROUND):
            if (step[0] == 0) == plane:
                pl.when(self.has(step))(lambda index=index: self.copy(index).start())

    def place(self, group, cell):
        return self.width * ((group * self.ny + cell[0]) * self.nx + cell[1])

    def start(self):
        width = self.width
        lane = lanes() // width
        last = first = jnp.zeros((16, L), F32)
        for cell in itertools.product(range(self.ny), range(self.nx)):
            row = self.field[cell[0] + 1, cell[1] + 1].astype(F32)
            for group in range(row.shape[0] // 16):
                piece = row[16 * group : 16 * group + 16]
                place = self.place(group, cell)
                here = lane == place // width
                last = jnp.where(here, pltpu.roll(piece, (place + width) % L, 1), last)
                first = jnp.where(here, pltpu.roll(piece, place, 1), first)
        self.sent[0] = last.astype(BF)
        self.sent[1] = first.astype(BF)
        self.start_where(False)
        self.start_where(True)

    def clear(self):
        zero = jnp.zeros(self.field.shape[2:], BF)
        for y in range(self.ny + 2):
            for x in range(self.nx + 2):
                if y in (0, self.ny + 1) or x in (0, self.nx + 1):
                    self.field[y, x] = zero
        self.edge[...] = jnp.zeros_like(self.edge)

    def wait(self):
        for index, step in enumerate(AROUND):
            pl.when(self.has(step, -1))(lambda index=index: self.copy(index).wait_recv())

    def wait_sent(self):
        for index, step in enumerate(AROUND):
            pl.when(self.has(step))(lambda index=index: self.copy(index).wait_send())

    def shift(self, low, high, by):
        ny, nx = self.ny, self.nx
        lane = lanes()
        for y in range(ny + 2):
            for x in range(nx + 2):
                row = self.field[y, x].astype(F32)
                (dy, oy), (dx, ox) = divmod(y + ny - 1, ny), divmod(x + nx - 1, nx)
                left = self.edge[0, dy * 3 + dx].astype(F32)
                right = self.edge[1, dy * 3 + dx].astype(F32)
                places = [self.place(group, (oy, ox)) for group in range(row.shape[0] // 16)]
                first = jnp.concatenate([pltpu.roll(left, (L - at) % L, 1) for at in places])
                last = jnp.concatenate([pltpu.roll(right, (2 * L - by - at) % L, 1) for at in places])
                low[y, x] = jnp.where(lane < by, first, pltpu.roll(row, by, 1)).astype(BF)
                high[y, x] = jnp.where(lane >= L - by, last, pltpu.roll(row, L - by, 1)).astype(BF)


def patch(low, mid, high, y, x):
    pieces = []
    for ref in (low, mid, high):
        for ky in range(3):
            for kx in range(3):
                pieces.append(ref(y + ky, x + kx))
    return jnp.concatenate(pieces, axis=0)


def reader(ref):
    return lambda y, x: ref[y, x]


class Total:
    def __init__(self, at, sizes, refs, sems, owners, each):
        self.at, self.sizes, self.owners, self.each = at, sizes, owners, each
        self.terms, self.landed, self.held, self.result = refs
        self.sems = sems
        self.me = at[1] * sizes[2] + at[2]
        self.count = sizes[1] * sizes[2]

    def whole(self):
        return self.owners == self.count

    def when_owner(self, device, action):
        if self.whole():
            action()
        else:
            pl.when(device < self.owners)(action)

    def target(self, step):
        return lax.rem(self.me + step, self.count)

    def device(self, index):
        return (self.at[0], index // self.sizes[2], lax.rem(index, self.sizes[2]))

    def chunk(self, index):
        return pl.ds(index * self.each, self.each)

    def drain(self, ref, copies, sem):
        if copies:
            span = ref.at[pl.ds(0, copies)]
            pltpu.make_async_copy(span, span, self.sems.at[sem]).wait()

    def by_role(self, mine, others):
        if self.whole():
            mine()
        else:
            pl.when(self.me < self.owners)(mine)
            pl.when(self.me >= self.owners)(others)

    def start_scatter(self):
        for step in range(1, self.count):
            index = self.target(step)

            def send(step=step, index=index):
                pltpu.make_async_remote_copy(
                    src_ref=self.terms.at[self.chunk(index)],
                    dst_ref=self.landed.at[step - 1],
                    send_sem=self.sems.at[0],
                    recv_sem=self.sems.at[1],
                    device_id=self.device(index),
                    device_id_type=MESH,
                ).start()

            self.when_owner(index, send)

    def start_exchange(self):
        slab = self.at[0]

        def act():
            self.drain(self.landed, self.count - 1, 1)
            total = self.terms[self.chunk(self.me)].astype(F32)
            for step in range(self.count - 1):
                total = total + self.landed[step].astype(F32)
            self.held[slab] = total.astype(BF)
            for step in range(1, self.sizes[0]):
                pltpu.make_async_remote_copy(
                    src_ref=self.held.at[slab],
                    dst_ref=self.held.at[slab],
                    send_sem=self.sems.at[2],
                    recv_sem=self.sems.at[3],
                    device_id=(lax.rem(slab + step, self.sizes[0]), self.at[1], self.at[2]),
                    device_id_type=MESH,
                ).start()

        self.when_owner(self.me, act)

    def start_gather(self):
        def act():
            self.drain(self.held, self.sizes[0] - 1, 3)
            total = self.held[0].astype(F32)
            for step in range(1, self.sizes[0]):
                total = total + self.held[step].astype(F32)
            self.result[self.chunk(self.me)] = total.astype(BF)
            for step in range(1, self.count):
                pltpu.make_async_remote_copy(
                    src_ref=self.result.at[self.chunk(self.me)],
                    dst_ref=self.result.at[self.chunk(self.me)],
                    send_sem=self.sems.at[4],
                    recv_sem=self.sems.at[5],
                    device_id=self.device(self.target(step)),
                    device_id_type=MESH,
                ).start()

        self.when_owner(self.me, act)

    def finish(self):
        def mine():
            self.drain(self.terms, (self.owners - 1) * self.each, 0)
            self.drain(self.held, self.sizes[0] - 1, 2)
            self.drain(self.landed, self.count - 1, 4)
            self.drain(self.result, (self.owners - 1) * self.each, 5)

        def others():
            self.drain(self.terms, self.owners * self.each, 0)
            self.drain(self.result, self.owners * self.each, 5)

        self.by_role(mine, others)


def kernel(
    sizes,
    plan,
    feat_in,
    cot_in,
    enc_in,
    down_in,
    dec_in,
    result_out,
    grad_feat_out,
    tiles_1_out,
    tiles_2_out,
    feat_ref,
    cot_ref,
    enc_ref,
    down_ref,
    dec_ref,
    result_ref,
    grad_feat_ref,
    rows_ref,
    w_enc,
    w_enc_t,
    w_down,
    w_down_t,
    w_dec,
    w_dec_t,
    fields,
    lows,
    highs,
    sents,
    edges,
    enc_pre,
    joined_grad,
    own_joined,
    dec_sum,
    dec_skip_sum,
    enc_sum,
    total_refs_1,
    total_refs_2,
    halo_send,
    halo_recv,
    total_sems,
    sems,
):
    (owners_1, each_1), (owners_2, each_2) = plan
    channels, nx, ny, _ = feat_ref.shape
    ncy = ny // 2
    coarse_channels = down_ref.shape[2]
    joined_channels = channels + coarse_channels
    at = (lax.axis_index("slab"), lax.axis_index("px"), lax.axis_index("py"))
    count = sizes[1] * sizes[2]
    sum_1 = Total(at, sizes, total_refs_1, total_sems.at[0], owners_1, each_1)
    sum_2 = Total(at, sizes, total_refs_2, total_sems.at[1], owners_2, each_2)

    arrive = [
        pltpu.make_async_copy(source, target, sems.at[index])
        for index, (source, target) in enumerate(
            zip((feat_in, cot_in, enc_in, down_in, dec_in), (feat_ref, cot_ref, enc_ref, down_ref, dec_ref))
        )
    ]
    for copy in arrive:
        copy.start()

    def halo(index, rows, columns, width):
        refs = (fields[index], sents[index], edges[index])
        return Halo(at, sizes, *refs, (halo_send.at[index], halo_recv.at[index]), rows, columns, width)

    halos = [halo(index, *((ny, nx, 1) if index in FINE else (ncy, 1, 2))) for index in range(7)]
    of_feat, of_cot, of_pool, of_skip, of_slope, of_coarse, of_back = halos
    for each in halos:
        each.clear()

    barrier = pltpu.get_barrier_semaphore()
    for step in range(1, count):
        pl.semaphore_signal(barrier, inc=1, device_id=sum_1.device(sum_1.target(step)), device_id_type=MESH)
    for step in range(1, sizes[0]):
        other = lax.rem(at[0] + step, sizes[0])
        pl.semaphore_signal(barrier, inc=1, device_id=(other, at[1], at[2]), device_id_type=MESH)
    greeted = count - 1 + sizes[0] - 1
    for step in AROUND:
        if step[0] and (step[1] or step[2]):
            there = near(at, sizes, step)
            greeted = greeted + there.astype(jnp.int32)
            target = tuple(a + d for a, d in zip(at, step))

            @pl.when(there)
            def _(target=target):
                pl.semaphore_signal(barrier, inc=1, device_id=target, device_id_type=MESH)

    across = nx * ny
    for index, ref in ((0, feat_ref), (1, cot_ref)):
        arrive[index].wait()
        rows_ref[...] = ref[...].astype(F32).reshape(channels * across, L)
        for x in range(nx):
            for y in range(ny):
                row = rows_ref[pl.ds(x * ny + y, channels, stride=across), :]
                fields[index][y + 1, x + 1] = row.astype(BF)
    terms_1, terms_2 = total_refs_1[0], total_refs_2[0]
    terms_1[...] = jnp.zeros_like(terms_1)
    terms_2[...] = jnp.zeros_like(terms_2)
    pl.semaphore_wait(barrier, greeted)

    of_feat.start()
    of_cot.start()
    for copy in arrive[2:]:
        copy.wait()
    w_enc[...] = jnp.concatenate([enc_ref[p] for p in PLACE], axis=1)
    w_enc_t[...] = jnp.concatenate([enc_ref[26 - p] for p in PLACE], axis=0).T
    w_down[...] = jnp.concatenate([down_ref[p] for p in PLACE], axis=0).T
    w_down_t[...] = jnp.concatenate([down_ref[26 - p] for p in PLACE], axis=1)
    w_dec[...] = jnp.concatenate([dec_ref[p] for p in PLACE], axis=1)
    w_dec_t[...] = jnp.concatenate([dec_ref[26 - p] for p in PLACE], axis=0).T

    def moved(index, by):
        halos[index].shift(lows[index], highs[index], by)
        return reader(lows[index]), reader(fields[index]), reader(highs[index])

    def fine(of, y):
        return jnp.concatenate([patch(*of, y, x) for x in range(nx)], axis=1)

    def span_of(y):
        return pl.ds(pl.multiple_of(y * (nx * L), nx * L), nx * L)

    of_feat.wait()
    feat_of = moved(0, 1)

    def encode(yc, carry):
        pooled = jnp.zeros((channels, L), F32)
        for sub in range(2):
            y = 2 * yc + sub
            pre = dot(w_enc[...], fine(feat_of, y))
            enc_pre[:, span_of(y)] = pre
            skip = (pre * jax.nn.sigmoid(pre)).astype(BF)
            own_joined[coarse_channels:, span_of(y)] = skip
            for x in range(nx):
                row = skip[:, x * L : (x + 1) * L]
                fields[3][y + 1, x + 1] = row
                pooled = pooled + row.astype(F32)
        fields[2][yc + 1, 1] = (pair_sum(pooled) * 0.125).astype(BF)
        return carry

    lax.fori_loop(0, ncy, encode, 0)

    of_pool.start()
    of_skip.start()
    of_cot.wait()
    cot_of = moved(1, 1)

    def back(y, carry):
        joined_grad[:, span_of(y)] = dot(w_dec_t[...], fine(cot_of, y))
        return carry

    lax.fori_loop(0, ny, back, 0)
    dec_skip_sum[...] = jnp.zeros_like(dec_skip_sum)

    def dec_skip_step(y, carry):
        dec_skip_sum[...] += dot_t(fine(cot_of, y), own_joined[coarse_channels:, span_of(y)])
        return carry

    lax.fori_loop(0, ny, dec_skip_step, 0)
    held_rows = 7 * channels
    quarters = [dec_skip_sum[q * held_rows : (q + 1) * held_rows] for q in range(3)]
    quarters.append(jnp.concatenate([dec_skip_sum[3 * held_rows :], jnp.zeros((channels, channels), F32)], axis=0))
    skip_tiles = jnp.concatenate(quarters, axis=1).astype(BF).reshape(held_rows // 16, 16, L)
    terms_2[terms_2.shape[0] - held_rows // 16 :] = skip_tiles
    of_pool.wait()
    pool_of = moved(2, 2)
    pooled_patch = jnp.concatenate([patch(*pool_of, yc, 0) for yc in range(ncy)], axis=1)
    down_pre = dot(w_down[...], pooled_patch)
    slope = silu_slope(down_pre)
    grads = []
    for yc in range(ncy):
        folded = jnp.zeros((coarse_channels, L), F32)
        for sub in range(2):
            for x in range(nx):
                cell = ((2 * yc + sub) * nx + x) * L
                folded = folded + joined_grad[:coarse_channels, cell : cell + L]
        grad = (pair_sum(folded) * slope[:, yc * L : (yc + 1) * L]).astype(BF)
        fields[4][yc + 1, 1] = grad
        grads.append(grad)

    of_slope.start()
    coarse = (down_pre * jax.nn.sigmoid(down_pre)).astype(BF)
    for yc in range(ncy):
        own = coarse[:, yc * L : (yc + 1) * L]
        fields[5][yc + 1, 1] = own
        for sub in range(2):
            for x in range(nx):
                cell = ((2 * yc + sub) * nx + x) * L
                own_joined[:coarse_channels, cell : cell + L] = own
    down_sum = dot_t(pooled_patch, jnp.concatenate(grads, axis=1)) * 0.5
    half = down_sum.shape[0] // 2
    dec_sum[...] = jnp.zeros_like(dec_sum)

    def dec_step(y, carry):
        dec_sum[...] += dot_t(fine(cot_of, y), own_joined[:coarse_channels, span_of(y)])
        return carry

    lax.fori_loop(0, ny, dec_step, 0)
    tiles = half // 16
    for index, value in enumerate((dec_sum[...], down_sum)):
        paired = jnp.concatenate([value[:half], value[half:]], axis=1)
        terms_1[index * tiles : (index + 1) * tiles] = paired.astype(BF).reshape(tiles, 16, L)
    sum_1.start_scatter()
    of_coarse.start()
    of_slope.wait()
    slope_of = moved(4, 2)
    slope_patch = jnp.concatenate([patch(*slope_of, yc, 0) for yc in range(ncy)], axis=1)
    grad_pooled = dot(w_down_t[...], slope_patch) * 0.125
    for yc in range(ncy):
        for sub in range(2):
            for x in range(nx):
                cell = ((2 * yc + sub) * nx + x) * L
                total = joined_grad[coarse_channels:, cell : cell + L] + grad_pooled[:, yc * L : (yc + 1) * L]
                grad = (total * silu_slope(enc_pre[:, cell : cell + L])).astype(BF)
                fields[6][2 * yc + sub + 1, x + 1] = grad

    enc_sum[...] = jnp.zeros_like(enc_sum)

    def enc_step(y, carry):
        own = jnp.concatenate([fields[6][y + 1, x + 1] for x in range(nx)], axis=1)
        enc_sum[...] += dot_t(own, fine(feat_of, y))
        return carry

    lax.fori_loop(0, ny, enc_step, 0)
    wide = enc_sum.shape[1]
    for h in range(channels // 16):
        for at_lane in range(0, wide, L):
            size = min(L, wide - at_lane)
            piece = enc_sum[16 * h : 16 * h + 16, at_lane : at_lane + size]
            terms_2[h * pl.cdiv(wide, L) + at_lane // L, :, 0:size] = piece.astype(BF)
    sum_2.start_scatter()
    of_back.start()
    def put(y, value):
        for x in range(nx):
            rows_ref[pl.ds(x * ny + y, channels, stride=across), :] = value[:, x * L : (x + 1) * L]

    leave = [
        pltpu.make_async_copy(source, target, sems.at[index])
        for index, (source, target) in enumerate(
            zip(
                (result_ref, grad_feat_ref, total_refs_1[3], total_refs_2[3]),
                (result_out, grad_feat_out, tiles_1_out, tiles_2_out),
            )
        )
    ]

    def flush(ref, copy):
        ref[...] = rows_ref[...].reshape(channels, nx, ny, L).astype(BF)
        copy.start()

    of_coarse.wait()
    coarse_of = moved(5, 1)
    of_skip.wait()
    skip_of = moved(3, 1)

    sum_1.start_exchange()
    def result_step(yc, carry):
        for sub in range(2):
            columns = []
            for x in range(nx):
                pieces = []
                for kz in range(3):
                    for ky in range(3):
                        for kx in range(3):
                            pieces.append(coarse_of[kz](yc + (sub + ky + 1) // 2, (x + kx + 1) // 2))
                            pieces.append(skip_of[kz](2 * yc + sub + ky, x + kx))
                columns.append(jnp.concatenate(pieces, axis=0))
            put(2 * yc + sub, dot(w_dec[...], jnp.concatenate(columns, axis=1)))
        return carry

    lax.fori_loop(0, ncy, result_step, 0)
    sum_2.start_exchange()
    flush(result_ref, leave[0])
    sum_1.start_gather()
    of_back.wait()
    back_of = moved(6, 1)
    def feat_step(y, carry):
        put(y, dot(w_enc_t[...], fine(back_of, y)))
        return carry

    lax.fori_loop(0, ny, feat_step, 0)
    sum_2.start_gather()
    flush(grad_feat_ref, leave[1])

    for each in halos:
        each.wait_sent()
    sum_1.finish()
    leave[2].start()
    sum_2.finish()
    leave[3].start()
    for copy in leave:
        copy.wait()


def unpack(
    scale,
    result_in,
    grad_feat_in,
    tiles_1_in,
    tiles_2_in,
    result_out,
    grad_feat_out,
    grad_enc_out,
    grad_down_out,
    grad_dec_out,
    result,
    grad_feat,
    tiles_1,
    tiles_2,
    grad_enc,
    grad_down,
    grad_dec,
    sems,
):
    arrived = [
        pltpu.make_async_copy(source, target, sems.at[index])
        for index, (source, target) in enumerate(zip((tiles_1_in, tiles_2_in, result_in, grad_feat_in), (tiles_1, tiles_2, result, grad_feat)))
    ]
    for copy in arrived:
        copy.start()
    ends = (result_out, grad_feat_out, grad_enc_out, grad_down_out, grad_dec_out)
    leaving = [
        pltpu.make_async_copy(source, target, sems.at[4 + index])
        for index, (source, target) in enumerate(zip((result, grad_feat, grad_enc, grad_down, grad_dec), ends))
    ]
    channels, coarse_channels = grad_down.shape[1:]
    tiles = channels // 16
    half = 27 * channels // 2

    def unpaired(index):
        span = tiles_1[index * (half // 16) : (index + 1) * (half // 16)]
        both = span.astype(F32).reshape(half, L) * scale
        return jnp.concatenate([both[:, :coarse_channels], both[:, coarse_channels:]], axis=0)

    arrived[0].wait()
    whole = unpaired(1)
    for index, place in enumerate(PLACE):
        grad_down[place] = whole[index * channels : (index + 1) * channels]
    leaving[3].start()
    whole = unpaired(0)
    arrived[1].wait()
    first = tiles_2.shape[0] - 7 * tiles
    for index, place in enumerate(PLACE):
        quarter, row = divmod(index, 7)
        span = tiles_2[first + row * tiles : first + (row + 1) * tiles]
        skip = span.astype(F32).reshape(channels, L)[:, quarter * channels : (quarter + 1) * channels]
        rows = whole[index * channels : (index + 1) * channels]
        grad_dec[26 - place] = jnp.concatenate([rows, skip * scale], axis=1)
    leaving[4].start()
    across_tiles = pl.cdiv(27 * channels, L)
    for index, place in enumerate(PLACE):
        lane = index * channels
        for h in range(tiles):
            tile = tiles_2[h * across_tiles + lane // L].astype(F32)
            grad_enc[place, 16 * h : 16 * h + 16] = tile[:, lane % L : lane % L + channels] * scale
    leaving[2].start()
    for index in (0, 1):
        arrived[2 + index].wait()
        leaving[index].start()
    for copy in leaving:
        copy.wait()


def shards(sizes, feat, w_enc, w_down, w_dec, cotangent):
    channels, nx, ny, nz = feat.shape
    coarse_channels = w_down.shape[0]
    joined_channels = channels + coarse_channels
    ncy = ny // 2
    count = sizes[1] * sizes[2]
    tiles_1 = 2 * (27 * channels // 32)
    tiles_2 = channels // 16 * pl.cdiv(27 * channels, L) + 7 * channels // 16
    each_1, each_2 = pl.cdiv(tiles_1, count), pl.cdiv(tiles_2, count)
    owners_1, owners_2 = pl.cdiv(tiles_1, each_1), pl.cdiv(tiles_2, each_2)

    def taps(weight, order):
        return weight.transpose(2, 3, 4, *order).reshape(27, weight.shape[order[0]], weight.shape[order[1]])

    def vmem(*shape, dtype=BF):
        return pltpu.VMEM(shape, dtype)

    def fine(c):
        return vmem(ny + 2, nx + 2, c, L)

    def small(c):
        return vmem(ncy + 2, 3, c, L)

    c1, c2, cj = channels, coarse_channels, joined_channels
    shaped = [fine(c1), fine(c1), small(c1), fine(c1), small(c2), small(c2), fine(c1)]
    scratch = [vmem(*feat.shape)] * 2
    scratch += [vmem(27, c1, c) for c in (c1, c2, cj)]
    scratch += [vmem(*feat.shape)] * 2
    scratch += [
        vmem(c1 * nx * ny, L, dtype=F32),
        vmem(c1, 27 * c1),
        vmem(c1, 27 * c1),
        vmem(c2, 27 * c1),
        vmem(c1, 27 * c2),
        vmem(c1, 27 * cj),
        vmem(cj, 27 * c1),
    ]
    scratch += [shaped] * 3
    scratch += [[vmem(2, 16, L)] * 7, [vmem(2, 9, 16, L)] * 7]
    scratch += [
        vmem(c1, nx * ny * L, dtype=F32),
        vmem(cj, nx * ny * L, dtype=F32),
        vmem(cj, nx * ny * L),
        vmem(27 * c1, c2, dtype=F32),
        vmem(27 * c1, c1, dtype=F32),
        vmem(c1, 27 * c1, dtype=F32),
    ]
    for owners, each in ((owners_1, each_1), (owners_2, each_2)):
        scratch.append(
            [
                vmem(owners * each, 16, L),
                vmem(count - 1, each, 16, L),
                vmem(sizes[0], each, 16, L),
                vmem(owners * each, 16, L),
            ]
        )
    scratch += [
        pltpu.SemaphoreType.DMA((7, len(AROUND))),
        pltpu.SemaphoreType.DMA((7, len(AROUND))),
        pltpu.SemaphoreType.DMA((2, 6)),
        pltpu.SemaphoreType.DMA((5,)),
    ]
    apart = pl.BlockSpec(memory_space=pl.ANY)
    fields = [jax.ShapeDtypeStruct(feat.shape, BF)] * 2
    grads = [jax.ShapeDtypeStruct((27, c1, c), F32) for c in (c1, c2, cj)]
    held_tiles = (owners_1 * each_1, owners_2 * each_2)
    tiles = [jax.ShapeDtypeStruct((size, 16, L), BF) for size in held_tiles]
    held = pl.pallas_call(
        functools.partial(kernel, sizes, ((owners_1, each_1), (owners_2, each_2))),
        out_shape=fields + tiles,
        in_specs=[apart] * 5,
        out_specs=[apart] * 4,
        scratch_shapes=scratch,
        compiler_params=pltpu.CompilerParams(
            collective_id=0, has_side_effects=True, vmem_limit_bytes=56 << 20
        ),
    )(feat, cotangent, taps(w_enc, (0, 1)), taps(w_down, (1, 0)), taps(w_dec, (0, 1)))
    scale = 1.0 / math.sqrt(float(nx * ny * nz * sizes[0] * sizes[1] * sizes[2]))
    result, grad_feat, grad_enc, grad_down, grad_dec = pl.pallas_call(
        functools.partial(unpack, scale),
        out_shape=fields + grads,
        in_specs=[apart] * 4,
        out_specs=[apart] * 5,
        scratch_shapes=[pltpu.VMEM(each.shape, each.dtype) for each in fields + tiles + grads]
        + [pltpu.SemaphoreType.DMA((9,))],
        compiler_params=pltpu.CompilerParams(vmem_limit_bytes=60 << 20),
    )(*held)

    def untaps(value, order):
        return value.reshape(3, 3, 3, *value.shape[1:]).transpose(*order, 0, 1, 2)

    return (
        result,
        grad_feat,
        untaps(grad_enc, (3, 4)),
        untaps(grad_down, (4, 3)),
        untaps(grad_dec, (3, 4)),
    )


def solution(mesh):
    sizes = tuple(mesh.shape[axis] for axis in ("slab", "px", "py"))
    placed = P(None, "px", "py", "slab")
    return jax.shard_map(
        functools.partial(shards, sizes),
        mesh=mesh,
        in_specs=(placed, P(), P(), P(), placed),
        out_specs=(placed, placed, P(), P(), P()),
        check_vma=False,
    )
```
